256 devices in a mesh: rows: 64 (over z, y_hi, x), rep: 4 (over y_lo, core).
Axes of the slice: x: 4, y: 4 (y_hi: 2, y_lo: 2; y = y_hi * 2 + y_lo), z: 8, core: 2. Of those that a mesh axis runs over, the one named last changes fastest.
Arguments:
- features: bfloat16 [49152, 256], P('rows'), may hold values from -6 to 6
- degrees: int32 [49152], P('rows'), may hold values from 1 to 8
- cotangent: bfloat16 [49152, 256], P('rows'), may hold values from -6 to 6
- self_weight: bfloat16 [256, 256], replicated, may hold values from -0.375 to 0.375
- neigh_weight: bfloat16 [256, 256], replicated, may hold values from -0.375 to 0.375
- bias_vector: bfloat16 [256], replicated, may hold values from -3 to 3
- block_values: bfloat16 [64, 64, 12, 128, 128], P('rows', 'rep'), may hold values from -0.14941406 to 0.14941406
- block_rows: int32 [64, 64, 12], P('rows', 'rep'), may hold values from 0 to 5
- block_cols: int32 [64, 64, 12], P('rows', 'rep'), may hold values from 0 to 5
- block_count: int32 [64, 64], P('rows', 'rep'), may hold values from 1 to 12, as said below
Outputs:
- output: bfloat16 [49152, 256], P(('rows', 'rep'))
- grad_input: bfloat16 [49152, 256], P(('rows', 'rep'))
The draws below stay inside these ranges and needn't reach their ends.
Inputs may be any that keep to these rules, and one draw needn't show every extreme that they name: block_count[p, d] is the number of live slots of row panel p at distance d; some pair holds 12 in every draw.
All inputs are finite; a program needn't handle non-finite values.
Results may differ from the reference program's by a relative error of at most 0.012.
Values may be sent and summed in bfloat16 or wider, within the bound.
A program may use at most 192 MiB of HBM per device.

```python
import jax
import jax.numpy as jnp
from jax import lax

HID = 256
BLK = 128
SLOTS = 12
ROW_BLOCKS = 6
PANELS = 64
SECTIONS = 16
NODES = 49152


def draw_block_count(key, part):
    key = jax.random.fold_in(key, 7)
    distance = jnp.arange(PANELS, dtype=jnp.int32)[None, :]
    ceiling = jnp.where(distance < SECTIONS, SLOTS + 1, max(SLOTS // 4, 1) + 1)
    ceiling = jnp.broadcast_to(ceiling, (PANELS, PANELS))
    counts = jax.random.randint(key, (PANELS, PANELS), 1, ceiling)
    counts = jnp.where(distance == 0, SLOTS, counts)
    return counts.astype(jnp.int32)


def place_ends(drawn, own_key, low, top_value):
    longest = drawn.shape.index(max(drawn.shape))
    spots = []
    for shift in (0, 1):
        where = [jax.random.randint(jax.random.fold_in(own_key, axis), (), 0, length) for axis, length in enumerate(drawn.shape)]
        where[longest] = (where[longest] + shift) % drawn.shape[longest]
        spots.append(tuple(where))
    return drawn.at[spots[0]].set(low).at[spots[1]].set(top_value)


def levels(rng, shape, cuts, low, top_value):
    factor_of, own = 1.0, jax.random.fold_in(rng, 6)
    for axis_at, shards_of in cuts:
        steps = jnp.exp(jax.random.uniform(jax.random.fold_in(own, axis_at), (shards_of,), jnp.float32, low / len(cuts), top_value / len(cuts)))
        factor_of = factor_of * jnp.repeat(steps, shape[axis_at] // shards_of).reshape([-1 if axis == axis_at else 1 for axis in range(len(shape))])
    return factor_of


def normal_values(own_key, shape, scale, most, split=(), kind=jnp.bfloat16):
    level = levels(own_key, shape, split, -0.22, 0.18) if split else 1.0
    values = jax.random.normal(own_key, shape, jnp.float32) * scale * level
    return jnp.minimum(jnp.maximum(values, -most), most).astype(kind)


def setup_inputs(seed: int = 0) -> dict:
    keys = jax.random.split(jax.random.key(seed), 11)
    features = normal_values(keys[0], (NODES, HID), 1.0, 6.0, ((0, 64),))
    degrees = place_ends(jax.random.randint(keys[1], (NODES,), 1, 9), jax.random.fold_in(keys[1], 1), 1, 8).astype(jnp.int32)
    cotangent = normal_values(keys[2], (NODES, HID), 1.0, 6.0, ((0, 64),))
    self_weight = normal_values(keys[3], (HID, HID), HID ** -0.5, 0.375)
    neigh_weight = normal_values(keys[4], (HID, HID), HID ** -0.5, 0.375)
    bias_vector = normal_values(keys[5], (HID,), 0.5, 3.0)
    block_values = normal_values(keys[6], (PANELS, PANELS, SLOTS, BLK, BLK), 0.025, 0.14941406, ((0, 64), (1, 4)))
    block_rows = place_ends(jax.random.randint(keys[7], (PANELS, PANELS, SLOTS), 0, ROW_BLOCKS), jax.random.fold_in(keys[7], 1), 0, ROW_BLOCKS - 1).astype(jnp.int32)
    block_cols = place_ends(jax.random.randint(keys[8], (PANELS, PANELS, SLOTS), 0, ROW_BLOCKS), jax.random.fold_in(keys[8], 1), 0, ROW_BLOCKS - 1).astype(jnp.int32)
    block_count = draw_block_count(jax.random.fold_in(keys[10], 71), 0)
    return dict(features=features, degrees=degrees, cotangent=cotangent, self_weight=self_weight, neigh_weight=neigh_weight, bias_vector=bias_vector, block_values=block_values, block_rows=block_rows, block_cols=block_cols, block_count=block_count)


def silu_slope(preact):
    sigmoid_value = jax.nn.sigmoid(preact)
    return sigmoid_value * (1.0 + preact * (1.0 - sigmoid_value))


def reference(features, degrees, cotangent, self_weight, neigh_weight, bias_vector, block_values, block_rows, block_cols, block_count):
    node_blocks = features.reshape(PANELS * ROW_BLOCKS, BLK, HID)
    slot_ids = jnp.arange(SLOTS, dtype=jnp.int32)
    panel_ids = jnp.arange(PANELS, dtype=jnp.int32)
    block_ids = jnp.arange(ROW_BLOCKS, dtype=jnp.int32)

    def aggregate(panel_id):
        source = (panel_id - panel_ids) % PANELS
        row_index = (source[:, None] * ROW_BLOCKS + block_cols[panel_id]).astype(jnp.int32)
        picked = node_blocks[row_index].astype(jnp.float32)
        weights = block_values[panel_id].astype(jnp.float32)
        product = jnp.einsum('dkij,dkjf->dkif', weights, picked, precision=lax.Precision.HIGHEST)
        live_mask = slot_ids[None, :] < block_count[panel_id][:, None]
        placement = ((block_rows[panel_id][None] == block_ids[:, None, None]) & live_mask[None]).astype(jnp.float32)
        return jnp.einsum('rdk,dkif->rif', placement, product, precision=lax.Precision.HIGHEST)

    agg = lax.map(aggregate, panel_ids).reshape(NODES, HID)
    divisor = degrees.astype(jnp.float32)[:, None]
    neighbours = (agg / divisor).astype(jnp.bfloat16)
    preact = jnp.dot(features, self_weight, preferred_element_type=jnp.float32)
    preact = preact + jnp.dot(neighbours, neigh_weight, preferred_element_type=jnp.float32)
    preact = preact + bias_vector.astype(jnp.float32)[None, :]
    output = jax.nn.silu(preact).astype(jnp.bfloat16)
    pre_grad = (cotangent.astype(jnp.float32) * silu_slope(preact)).astype(jnp.bfloat16)
    scaled = (jnp.dot(pre_grad, neigh_weight.T, preferred_element_type=jnp.float32) / divisor).astype(jnp.bfloat16)
    scaled_blocks = scaled.reshape(PANELS * ROW_BLOCKS, BLK, HID)

    def spread(running, panel_id):
        source = (panel_id - panel_ids) % PANELS
        picked = scaled_blocks[(panel_id * ROW_BLOCKS + block_rows[panel_id]).astype(jnp.int32)].astype(jnp.float32)
        weights = block_values[panel_id].astype(jnp.float32)
        product = jnp.einsum('dkji,dkjf->dkif', weights, picked, precision=lax.Precision.HIGHEST)
        live_mask = (slot_ids[None, :] < block_count[panel_id][:, None]).astype(jnp.float32)
        product = product * live_mask[:, :, None, None]
        target = (source[:, None] * ROW_BLOCKS + block_cols[panel_id]).astype(jnp.int32)
        running = running.at[target.reshape(-1)].add(product.reshape(PANELS * SLOTS, BLK, HID))
        return running, None

    back, unused = lax.scan(spread, jnp.zeros((PANELS * ROW_BLOCKS, BLK, HID), jnp.float32), panel_ids)
    grad_input = jnp.dot(pre_grad, self_weight.T, preferred_element_type=jnp.float32) + back.reshape(NODES, HID)
    return output, grad_input.astype(jnp.bfloat16)
```

```python
import jax
import jax.numpy as jnp
from jax import lax
from jax.experimental import pallas as pl
from jax.experimental.pallas import tpu as pltpu
from jax.sharding import PartitionSpec as P

MESH = pl.DeviceIdType.MESH
F32 = jnp.float32
BF16 = jnp.bfloat16
NB = 6
BLK = 128
SLOTS = 12
PR = NB * BLK
HALF = PR // 2
HID = 256
QR = PR // 4


class Copies:
    def __init__(self, send_sems, recv_sems):
        self.send_sems, self.recv_sems = send_sems, recv_sems
        self.sends = 0
        self.recvs = 0
        self.pending = []

    def recv_slot(self):
        self.recvs += 1
        return self.recvs - 1

    def start(self, src, dst, recv_slot, device, cond=None, send_slot=None, track=True):
        if send_slot is None:
            send_slot = self.sends
            self.sends += 1
        copy = pltpu.make_async_remote_copy(
            src_ref=src,
            dst_ref=dst,
            send_sem=self.send_sems.at[send_slot],
            recv_sem=self.recv_sems.at[recv_slot],
            device_id=device,
            device_id_type=MESH,
        )
        if cond is None:
            copy.start()
        else:
            pl.when(cond)(lambda: copy.start())
        if track:
            self.pending.append((cond, copy))
        return send_slot

    def wait_recv(self, ref, recv_slot):
        pltpu.make_async_copy(ref, ref, self.recv_sems.at[recv_slot]).wait()

    def drain(self):
        for cond, copy in self.pending:
            if cond is None:
                copy.wait_send()
            else:
                pl.when(cond)(lambda copy=copy: copy.wait_send())
        self.pending = []


def kernel(
    rows_s, cols_s, cnt_s, feat, deg, cot_hbm, wself, wneigh, bias, w_hbm,
    out, grad,
    wv, wt, xbuf, zbuf, acc, lhs, rhs, stage, sstage, cot,
    mid_src, mid_in, sbuf, base,
    pbuf, opp_in, dir_in, znear, zfar, zone, chain_in, chain_out, fin_in,
    send_sems, recv_sems, load_sems, go_sem,
):
    i = lax.axis_index("rows")
    r = lax.axis_index("rep")
    z, yh, x, w = i // 8, lax.rem(i // 4, 2), lax.rem(i, 4), lax.rem(i, 8)
    lo, core = r // 2, lax.rem(r, 2)
    role = lax.rem(core + lo, 2)
    step = 1 - 2 * lo
    znext, zprev = lax.rem(z + step + 8, 8), lax.rem(z - step + 8, 8)
    xr, xl, xo = lax.rem(x + 1, 4), lax.rem(x + 3, 4), lax.rem(x + 2, 4)
    inner = jnp.logical_or(x == 1, x == 2)
    near_role, far_role = role == 0, role == 1

    def dev(z_, yh_, x_, lo_, role_):
        return (z_ * 8 + yh_ * 4 + x_, 2 * lo_ + lax.rem(role_ + lo_, 2))

    left, right = dev(z, yh, xl, lo, role), dev(z, yh, xr, lo, role)
    ahead, behind = dev(znext, yh, x, lo, role), dev(zprev, yh, x, lo, role)
    mate = dev(z, yh, x, lo, 1 - role)
    across = dev(z, 1 - yh, x, 1 - lo, role)

    def near(wp, w_at):
        return lax.rem(jnp.where(wp <= w_at, 1, 0) + lo, 2)

    load_w = pltpu.make_async_copy(w_hbm.at[0], wv, load_sems.at[0])
    load_w.start()
    load_cot = pltpu.make_async_copy(cot_hbm.at[pl.ds(r * QR, QR)], cot, load_sems.at[1])
    load_cot.start()

    barrier = pltpu.get_barrier_semaphore()
    partners = [left, right, ahead, behind]
    for other in range(1, 8):
        at = lax.rem(yh * 4 + r + other, 8)
        partners.append((z * 8 + (at // 4) * 4 + x, lax.rem(at, 4)))
    for partner in partners:
        pl.semaphore_signal(barrier, inc=1, device_id=partner, device_id_type=MESH)
    pl.semaphore_wait(barrier, len(partners))

    net = Copies(send_sems, recv_sems)
    order = (yh, 1 - yh)

    r_z0 = [net.recv_slot() for _ in order]
    r_z1 = [net.recv_slot() for _ in order]
    r_z2 = [net.recv_slot() for _ in order]
    r_dir = [[[net.recv_slot() for _ in range(2)] for _ in order] for _ in range(2)]
    r_opp = [[[net.recv_slot() for _ in range(2)] for _ in order] for _ in range(2)]

    def comp_direct(o, hh, idx, slots):
        for side, (nx, target) in enumerate(((xr, right), (xl, left))):
            flag = near(4 * hh + x, 4 * yh + nx)
            cond = flag == (1 if idx == 0 else 0)
            slots[side] = net.start(
                zbuf.at[idx, hh], xbuf.at[0, hh, x], r_dir[0][o][side], target,
                cond=cond, send_slot=slots[side], track=True,
            )

    @pl.when(near_role)
    def _():
        zbuf[0, yh] = feat[...]

    net.start(feat, zbuf.at[0, yh], r_z0[1], across, cond=near_role)
    comp_slots = [[None, None], [None, None]]
    for o, hh in enumerate(order):
        if o == 0:
            @pl.when(far_role)
            def _(o=o, hh=hh):
                net.wait_recv(zbuf.at[0, hh], r_z0[o])
        else:
            net.wait_recv(zbuf.at[0, hh], r_z0[o])
        net.start(zbuf.at[0, hh], xbuf.at[1, hh, x], r_z1[o], ahead)
        comp_direct(o, hh, 0, comp_slots[o])

    for o, hh in enumerate(order):
        net.wait_recv(xbuf.at[1, hh, x], r_z1[o])
        net.start(xbuf.at[1, hh, x], zbuf.at[1, hh], r_z2[o], ahead)
        net.start(xbuf.at[1, hh, x], xbuf.at[1, hh, x], r_dir[1][o][0], right)
        net.start(xbuf.at[1, hh, x], xbuf.at[1, hh, x], r_dir[1][o][1], left)

    load_w.wait()
    acc[...] = jnp.zeros_like(acc)

    def block_of(cl, hh, xs):
        wp = 4 * hh + xs
        if cl == 1:
            return 8 + w - wp
        return lax.rem(w - wp + 16, 16)

    def fill(j, blocks, src, source_ids, target_ids, transpose):
        count = cnt_s[0, j]
        for k in range(SLOTS):
            rhs[pl.ds(k * BLK, BLK), :] = src[source_ids[0, j, k]]
        for k in range(SLOTS):
            a = blocks[j, k]
            if transpose:
                wt[j, k] = a.T
            target = jnp.where(k < count, target_ids[0, j, k], -1)
            for b in range(NB):
                lhs[pl.ds(b * BLK, BLK), pl.ds(k * BLK, BLK)] = jnp.where(
                    target == b, a, jnp.zeros_like(a)
                )

    def forward(cl, xs_list):
        def body(t, carry):
            hh = lax.rem(t, 2)
            xs = xs_list[0]
            for n in range(1, len(xs_list)):
                xs = jnp.where(t // 2 == n, xs_list[n], xs)
            for b in range(NB):
                stage[b] = xbuf[cl, hh, xs, pl.ds(b * BLK, BLK), :]
            fill(block_of(cl, hh, xs), wv, stage, cols_s, rows_s, True)
            acc[...] += jnp.dot(lhs[...], rhs[...], preferred_element_type=F32)
            return carry

        lax.fori_loop(0, 2 * len(xs_list), body, 0)

    forward(1, [x])

    def pass_opposite(cl, o, hh):
        if cl == 0 and o == 0:
            net.wait_recv(xbuf.at[cl, hh, xl], r_dir[cl][o][0])
            net.start(xbuf.at[cl, hh, xl], xbuf.at[cl, hh, xl], r_opp[cl][o][0], right, cond=inner)
            net.wait_recv(xbuf.at[cl, hh, xr], r_dir[cl][o][1])
            net.start(xbuf.at[cl, hh, xr], xbuf.at[cl, hh, xr], r_opp[cl][o][0], left, cond=inner)
        else:
            a, b = pl.ds(0, HALF), pl.ds(HALF, HALF)
            net.wait_recv(xbuf.at[cl, hh, xl], r_dir[cl][o][0])
            net.start(xbuf.at[cl, hh, xl, a], xbuf.at[cl, hh, xl, a], r_opp[cl][o][0], right)
            net.wait_recv(xbuf.at[cl, hh, xr], r_dir[cl][o][1])
            net.start(xbuf.at[cl, hh, xr, b], xbuf.at[cl, hh, xr, b], r_opp[cl][o][1], left)

    def wait_opposite(cl, o, hh):
        if cl == 0 and o == 0:
            net.wait_recv(xbuf.at[cl, hh, xo], r_opp[cl][o][0])
        else:
            net.wait_recv(xbuf.at[cl, hh, xo, pl.ds(0, HALF)], r_opp[cl][o][0])
            net.wait_recv(xbuf.at[cl, hh, xo, pl.ds(HALF, HALF)], r_opp[cl][o][1])

    for o, hh in enumerate(order):
        pass_opposite(1, o, hh)
        net.wait_recv(zbuf.at[1, hh], r_z2[o])
        net.start(zbuf.at[1, hh], zbuf.at[0, hh], r_z0[o], mate, cond=near_role)
        comp_direct(o, hh, 1, comp_slots[o])
        own = near(4 * hh + x, w)
        xbuf[0, hh, x] = zbuf[1 - own, hh]

    forward(1, [xl, xr])
    for o, hh in enumerate(order):
        pass_opposite(0, o, hh)
    for o, hh in enumerate(order):
        wait_opposite(1, o, hh)
    forward(1, [xo])
    forward(0, [x, xl, xr])
    for o, hh in enumerate(order):
        wait_opposite(0, o, hh)
    forward(0, [xo])

    mid_src[...] = acc[...].astype(BF16)
    r_mid, r_sc = net.recvs, net.recvs + 4
    net.recvs += 8
    peers = [lax.rem(r + n, 4) for n in range(1, 4)]
    for peer in peers:
        net.start(
            mid_src.at[pl.ds(pl.multiple_of(peer * QR, QR), QR)], mid_in.at[r], r_mid + r, (i, peer)
        )
    own_rows = pl.ds(pl.multiple_of(r * QR, QR), QR)
    total = acc[own_rows, :]
    f_own = feat[own_rows, :]
    divisor = deg[...]
    divisor = jnp.concatenate([divisor, divisor], axis=1)
    preact = jnp.dot(f_own, wself[...], preferred_element_type=F32) + bias[...]
    load_cot.wait()
    for peer in peers:
        net.wait_recv(mid_in.at[peer], r_mid + peer)
        total = total + mid_in[peer].astype(F32)
    neighbours = (total / divisor).astype(BF16)
    preact = preact + jnp.dot(neighbours, wneigh[...], preferred_element_type=F32)
    sig = jax.nn.sigmoid(preact)
    slope = sig * (1.0 + preact * (1.0 - sig))
    pre_grad = (cot[...].astype(F32) * slope).astype(BF16)
    contract = (((1,), (1,)), ((), ()))
    scaled = lax.dot_general(pre_grad, wneigh[...], contract, preferred_element_type=F32)
    sbuf[own_rows, :] = (scaled / divisor).astype(BF16)
    for peer in peers:
        net.start(sbuf.at[own_rows], sbuf.at[own_rows], r_sc + r, (i, peer))
    out[...] = (preact * sig).astype(BF16)
    base[...] = lax.dot_general(pre_grad, wself[...], contract, preferred_element_type=F32)
    for peer in peers:
        net.wait_recv(sbuf.at[pl.ds(pl.multiple_of(peer * QR, QR), QR)], r_sc + peer)
    for b in range(NB):
        sstage[b] = sbuf[pl.ds(b * BLK, BLK), :]

    b_opp = [[net.recvs + 4 * cl + 2 * o for o in range(2)] for cl in range(2)]
    net.recvs += 8
    b_dir = [[[net.recv_slot() for _ in range(2)] for _ in order] for _ in range(2)]
    b_chain = [[net.recv_slot() for _ in order] for _ in range(3)]

    def backward(cl, xs_list):
        def body(t, carry):
            hh = lax.rem(t, 2)
            xs = xs_list[0]
            for n in range(1, len(xs_list)):
                xs = jnp.where(t // 2 == n, xs_list[n], xs)
            fill(block_of(cl, hh, xs), wt, sstage, rows_s, cols_s, False)
            pbuf[cl, hh, xs] = jnp.dot(lhs[...], rhs[...], preferred_element_type=F32).astype(BF16)
            return carry

        lax.fori_loop(0, 2 * len(xs_list), body, 0)

    low, high = pl.ds(0, HALF), pl.ds(HALF, HALF)

    def send_opposite(cl):
        for o, hh in enumerate(order):
            if cl == 0 and o == 0:
                side = jnp.where(x <= 1, 0, 1)
                target = dev(z, yh, jnp.where(x <= 1, xr, xl), lo, role)
                net.start(pbuf.at[cl, hh, xo], opp_in.at[cl, o, side], b_opp[cl][o] + side, target)
            else:
                net.start(pbuf.at[cl, hh, xo, low], opp_in.at[cl, o, 1, low], b_opp[cl][o] + 1, left)
                net.start(pbuf.at[cl, hh, xo, high], opp_in.at[cl, o, 0, high], b_opp[cl][o], right)

    def send_direct(cl):
        for o, hh in enumerate(order):
            def merge(side, xs, part, o=o, hh=hh):
                net.wait_recv(opp_in.at[cl, o, side, part], b_opp[cl][o] + side)
                pbuf[cl, hh, xs, part, :] = (
                    pbuf[cl, hh, xs, part, :].astype(F32) + opp_in[cl, o, side, part, :].astype(F32)
                ).astype(BF16)

            if cl == 0 and o == 0:
                @pl.when(inner)
                def _(merge=merge):
                    merge(0, xr, pl.ds(0, PR))
                    merge(1, xl, pl.ds(0, PR))
            else:
                merge(0, xr, high)
                merge(1, xl, low)
            net.start(pbuf.at[cl, hh, xl], dir_in.at[cl, o, 1], b_dir[cl][o][1], left)
            net.start(pbuf.at[cl, hh, xr], dir_in.at[cl, o, 0], b_dir[cl][o][0], right)

    backward(0, [xo, xl, xr])

    @pl.when(near_role)
    def _():
        pl.semaphore_wait(go_sem, 1)

    send_opposite(0)
    backward(1, [xo])
    send_direct(0)
    send_opposite(1)
    backward(1, [xl, xr])
    send_direct(1)

    @pl.when(far_role)
    def _():
        pl.semaphore_signal(go_sem, inc=1, device_id=mate, device_id_type=MESH)

    backward(0, [x])
    for o, hh in enumerate(order):
        net.wait_recv(dir_in.at[0, o, 0], b_dir[0][o][0])
        net.wait_recv(dir_in.at[0, o, 1], b_dir[0][o][1])
        wp = 4 * hh + x
        n_own = near(wp, w).astype(F32)
        n_left = near(wp, 4 * yh + xl).astype(F32)
        n_right = near(wp, 4 * yh + xr).astype(F32)
        v_own = pbuf[0, hh, x].astype(F32)
        v_left = dir_in[0, o, 0].astype(F32)
        v_right = dir_in[0, o, 1].astype(F32)
        znear[o] = n_own * v_own + n_left * v_left + n_right * v_right
        far = (1.0 - n_own) * v_own + (1.0 - n_left) * v_left + (1.0 - n_right) * v_right
        zfar[o] = far

        @pl.when(far_role)
        def _(o=o, far=far):
            chain_out[2, o] = far.astype(BF16)

        net.start(chain_out.at[2, o], chain_in.at[1, o], b_chain[1][o], behind, cond=far_role)
    backward(1, [x])
    for o, hh in enumerate(order):
        net.wait_recv(dir_in.at[1, o, 0], b_dir[1][o][0])
        net.wait_recv(dir_in.at[1, o, 1], b_dir[1][o][1])
        zone[o] = (
            pbuf[1, hh, x].astype(F32) + dir_in[1, o, 0].astype(F32) + dir_in[1, o, 1].astype(F32)
        )
    for o in range(2):
        @pl.when(near_role)
        def _(o=o):
            net.wait_recv(chain_in.at[2, o], b_chain[2][o])
            chain_out[2, o] = (zfar[o] + chain_in[2, o].astype(F32)).astype(BF16)

        net.start(chain_out.at[2, o], chain_in.at[1, o], b_chain[1][o], behind, cond=near_role)
    for o in range(2):
        net.wait_recv(chain_in.at[1, o], b_chain[1][o])
        chain_out[1, o] = (zone[o] + chain_in[1, o].astype(F32)).astype(BF16)
        net.start(chain_out.at[1, o], chain_in.at[0, o], b_chain[0][o], behind)
    r_fin = net.recvs
    net.recvs += 4
    mine = 2 * lo + yh
    for o, hh in enumerate(order):
        net.wait_recv(chain_in.at[0, o], b_chain[0][o])
        chain_out[0, o] = (znear[o] + chain_in[0, o].astype(F32)).astype(BF16)
        net.start(chain_out.at[0, o], chain_in.at[2, o], b_chain[2][o], mate, cond=far_role)
        for quarter in range(4):
            rows = pl.ds(quarter * QR, QR)
            if o == 0:
                away = jnp.logical_and(near_role, r != quarter)

                @pl.when(jnp.logical_and(near_role, r == quarter))
                def _(rows=rows, o=o):
                    fin_in[mine] = chain_out[0, o, rows, :]
            else:
                away = near_role
            net.start(
                chain_out.at[0, o, rows], fin_in.at[mine], r_fin + mine, (z * 8 + hh * 4 + x, quarter),
                cond=away,
            )
    result = base[...]
    for source in range(4):
        @pl.when(jnp.logical_or(far_role, mine != source))
        def _(source=source):
            net.wait_recv(fin_in.at[source], r_fin + source)

    for source in range(4):
        result = result + fin_in[source].astype(F32)
    grad[...] = result.astype(BF16)
    net.drain()


def on_device(
    features, degrees, cotangent, self_weight, neigh_weight, bias_vector,
    block_values, block_rows, block_cols, block_count,
):
    r = lax.axis_index("rep")
    deg = lax.dynamic_slice_in_dim(degrees, r * QR, QR, 0).astype(F32)
    deg = jnp.broadcast_to(deg[:, None], (QR, BLK))
    vmem = pl.BlockSpec(memory_space=pltpu.VMEM)
    smem = pl.BlockSpec(memory_space=pltpu.SMEM)
    anyspace = pl.BlockSpec(memory_space=pl.ANY)
    panel = (PR, HID)
    return pl.pallas_call(
        kernel,
        out_shape=(
            jax.ShapeDtypeStruct((QR, HID), BF16),
            jax.ShapeDtypeStruct((QR, HID), BF16),
        ),
        in_specs=[smem, smem, smem, vmem, vmem, anyspace, vmem, vmem, vmem, anyspace],
        out_specs=(vmem, vmem),
        scratch_shapes=[
            pltpu.VMEM((16, SLOTS, BLK, BLK), BF16),
            pltpu.VMEM((16, SLOTS, BLK, BLK), BF16),
            pltpu.VMEM((2, 2, 4) + panel, BF16),
            pltpu.VMEM((2, 2) + panel, BF16),
            pltpu.VMEM(panel, F32),
            pltpu.VMEM((PR, SLOTS * BLK), BF16),
            pltpu.VMEM((SLOTS * BLK, HID), BF16),
            pltpu.VMEM((NB, BLK, HID), BF16),
            pltpu.VMEM((NB, BLK, HID), BF16),
            pltpu.VMEM((QR, HID), BF16),
            pltpu.VMEM(panel, BF16),
            pltpu.VMEM((4, QR, HID), BF16),
            pltpu.VMEM(panel, BF16),
            pltpu.VMEM((QR, HID), F32),
            pltpu.VMEM((2, 2, 4) + panel, BF16),
            pltpu.VMEM((2, 2, 2) + panel, BF16),
            pltpu.VMEM((2, 2, 2) + panel, BF16),
            pltpu.VMEM((2,) + panel, F32),
            pltpu.VMEM((2,) + panel, F32),
            pltpu.VMEM((2,) + panel, F32),
            pltpu.VMEM((3, 2) + panel, BF16),
            pltpu.VMEM((3, 2) + panel, BF16),
            pltpu.VMEM((4, QR, HID), BF16),
            pltpu.SemaphoreType.DMA((96,)),
            pltpu.SemaphoreType.DMA((96,)),
            pltpu.SemaphoreType.DMA((2,)),
            pltpu.SemaphoreType.REGULAR,
        ],
        compiler_params=pltpu.CompilerParams(
            collective_id=0, has_side_effects=True, vmem_limit_bytes=60 * 1024 * 1024
        ),
        name="sage_layer",
    )(
        block_rows, block_cols, block_count, features, deg, cotangent,
        self_weight, neigh_weight, bias_vector.astype(F32)[None, :], block_values,
    )


def solution(mesh):
    return jax.shard_map(
        on_device,
        mesh=mesh,
        in_specs=(
            P("rows", None),
            P("rows"),
            P("rows", None),
            P(),
            P(),
            P(),
            P("rows", "rep", None, None, None),
            P("rows", "rep", None),
            P("rows", "rep", None),
            P("rows", "rep"),
        ),
        out_specs=(P(("rows", "rep"), None), P(("rows", "rep"), None)),
        check_vma=False,
    )
```

```python
import jax
import jax.numpy as jnp
from jax import lax
from jax.experimental import pallas as pl
from jax.experimental.pallas import tpu as pltpu
from jax.sharding import PartitionSpec as P

MESH = pl.DeviceIdType.MESH
F32 = jnp.float32
BF16 = jnp.bfloat16
NB = 6
BLK = 128
SLOTS = 12
PR = NB * BLK
HID = 256
QR = PR // 4
RB = 80
AR = PR - 4 * RB
HA = AR // 2
FWD_STEPS = 46
BWD_STEPS = 46
BWD_LATE = 10


def quarter_parts(start, size):
    parts = []
    for quarter in range(4):
        a, b = max(start, quarter * QR), min(start + size, (quarter + 1) * QR)
        if a < b:
            parts.append((a - start, b - a, quarter, a - quarter * QR))
    return parts


A_PARTS = quarter_parts(0, AR)
B_PARTS = [quarter_parts(AR + q * RB, RB) for q in range(4)]


def kernel(
    rows_s, cols_s, cnt_s, feat, deg, cot_hbm, wself, wneigh, bias, w_hbm,
    out, grad,
    wv, wt, xbuf, zbuf, acc, lhs, rhs, stage, sstage, cot, dcol,
    mid_src, mid_in, sbuf, base, rbuf,
    pbuf, opp_in, dir_in, znear, zfar, zone, chain_in, chain_out, fin_a,
    rin, tin, tout, tacc, fin_b,
    send_sems, recv_sems, load_sems, go_sem,
    s_rz, r_rz, s_src, s_y, r_y, s_p, r_p, s_t, r_t, s_fb, r_fb,
):
    i = lax.axis_index("rows")
    r = lax.axis_index("rep")
    z, yh, x, w = i // 8, lax.rem(i // 4, 2), lax.rem(i, 4), lax.rem(i, 8)
    lo, core = r // 2, lax.rem(r, 2)
    role = lax.rem(core + lo, 2)
    step = 1 - 2 * lo
    znext, zprev = lax.rem(z + step + 8, 8), lax.rem(z - step + 8, 8)
    xr, xl, xo = lax.rem(x + 1, 4), lax.rem(x + 3, 4), lax.rem(x + 2, 4)
    inner = jnp.logical_or(x == 1, x == 2)
    near_role, far_role = role == 0, role == 1
    relay = 2 * yh + role
    share = pl.ds(pl.multiple_of(AR + RB * relay, 16), RB)
    share_across = pl.ds(pl.multiple_of(AR + RB * (2 * (1 - yh) + role), 16), RB)

    def dev(z_, yh_, x_, lo_, role_):
        return (z_ * 8 + yh_ * 4 + x_, 2 * lo_ + lax.rem(role_ + lo_, 2))

    left, right = dev(z, yh, xl, lo, role), dev(z, yh, xr, lo, role)
    opposite = dev(z, yh, xo, lo, role)
    ahead, behind = dev(znext, yh, x, lo, role), dev(zprev, yh, x, lo, role)
    mate = dev(z, yh, x, lo, 1 - role)
    across = dev(z, 1 - yh, x, 1 - lo, role)

    def near(wp, w_at, lo_at=lo):
        return lax.rem(jnp.where(wp <= w_at, 1, 0) + lo_at, 2)

    load_w = pltpu.make_async_copy(w_hbm.at[0], wv, load_sems.at[0])
    load_w.start()
    load_cot = pltpu.make_async_copy(cot_hbm.at[pl.ds(r * QR, QR)], cot, load_sems.at[1])
    load_cot.start()

    barrier = pltpu.get_barrier_semaphore()

    def greet(n, carry):
        at = lax.rem(w * 4 + r + n, 32)
        pl.semaphore_signal(
            barrier, inc=1, device_id=(z * 8 + at // 4, lax.rem(at, 4)), device_id_type=MESH
        )
        return carry

    lax.fori_loop(1, 32, greet, 0)
    pl.semaphore_signal(barrier, inc=1, device_id=ahead, device_id_type=MESH)
    pl.semaphore_signal(barrier, inc=1, device_id=behind, device_id_type=MESH)
    pl.semaphore_wait(barrier, 33)

    sends, recvs, pending = [0], [0], []

    def recv_slot(n=1):
        recvs[0] += n
        return recvs[0] - n

    def copy_to(src, dst, send_sem, recv_sem, device):
        return pltpu.make_async_remote_copy(
            src_ref=src, dst_ref=dst, send_sem=send_sem, recv_sem=recv_sem,
            device_id=device, device_id_type=MESH,
        )

    def joined(cond, role_cond):
        if cond is None or role_cond is None:
            return role_cond if cond is None else cond
        return jnp.logical_and(cond, role_cond)

    def start(src, dst, slot, device, cond=None, role_cond=None, send_slot=None):
        if send_slot is None:
            send_slot = sends[0]
            sends[0] += 1
        copy = copy_to(src, dst, send_sems.at[send_slot], recv_sems.at[slot], device)
        both = joined(cond, role_cond)
        if both is None:
            copy.start()
        else:
            pl.when(both)(lambda: copy.start())
        pending.append((cond, role_cond, src.shape[-2], send_slot))
        return send_slot

    def wait_bytes(ref, sem):
        pltpu.make_async_copy(ref, ref, sem).wait()

    def wait_recv(ref, slot):
        wait_bytes(ref, recv_sems.at[slot])

    def drain():
        for cond, role_cond, rows, slot in pending:
            cond = joined(cond, role_cond)

            def wait(rows=rows, slot=slot):
                wait_bytes(zbuf.at[0, 0, pl.ds(0, rows)], send_sems.at[slot])

            if cond is None:
                wait()
            else:
                pl.when(cond)(wait)
        pending.clear()

    def drain_many(sems, count, rows):
        def wait(n, carry):
            wait_bytes(zbuf.at[0, 0, pl.ds(0, rows)], sems.at[n])
            return carry

        lax.fori_loop(0, count, wait, 0)

    order = (yh, 1 - yh)
    arows = pl.ds(0, AR)
    low, high = pl.ds(0, HA), pl.ds(HA, HA)

    not_quarter = [r != quarter for quarter in range(4)]
    near_side = [
        [near(4 * hh + x, 4 * yh + nx) == 1 for nx in (xr, xl)] for hh in order
    ]
    far_side = [
        [near(4 * hh + x, 4 * yh + nx) == 0 for nx in (xr, xl)] for hh in order
    ]

    r_z0 = [recv_slot() for _ in order]
    r_z1 = [recv_slot() for _ in order]
    r_z2 = [recv_slot() for _ in order]
    r_dir = [[[recv_slot() for _ in range(2)] for _ in order] for _ in range(2)]
    r_opp = [[[recv_slot() for _ in range(2)] for _ in order] for _ in range(2)]
    comp_slots = [[None, None], [None, None]]

    def comp_direct(o, hh, idx, src, role_cond=None):
        flags = near_side if idx == 0 else far_side
        for side, target in enumerate((right, left)):
            comp_slots[o][side] = start(
                src, xbuf.at[0, hh, x, arows], r_dir[0][o][side], target,
                cond=flags[o][side], role_cond=role_cond, send_slot=comp_slots[o][side],
            )

    own_a = feat.at[arows]
    start(own_a, xbuf.at[1, yh, x, arows], r_z1[0], ahead, role_cond=near_role)
    start(own_a, zbuf.at[0, yh], r_z0[1], across, role_cond=near_role)
    own_b = feat.at[share]
    copy_to(own_b, rbuf.at[1, yh, x], s_rz.at[0], r_rz.at[8], behind).start()
    copy_to(feat.at[share_across], rbuf.at[0, yh, x], s_src.at[0], r_rz.at[1], across).start()
    for n, (target, at) in enumerate(((right, 2), (left, 3), (opposite, 4))):
        copy_to(own_b, rbuf.at[0, yh, x], s_src.at[1 + n], r_rz.at[at], target).start()
    comp_direct(0, yh, 0, own_a, near_role)

    @pl.when(near_role)
    def _():
        zbuf[0, yh] = feat[arows, :]

    rbuf[0, yh, x] = feat[share, :]

    dcol_rows = deg[...].astype(F32)
    dcol_t = jnp.concatenate([dcol_rows, dcol_rows[0:2]], axis=0).T
    for b in range(NB):
        dcol[pl.ds(b * BLK, BLK), :] = jnp.broadcast_to(dcol_t[:, b : b + 1], (BLK, HID))

    acc[...] = jnp.zeros_like(acc)
    load_w.wait()

    def block_of(cl, wp):
        return jnp.where(cl == 1, 8 + w - wp, lax.rem(w - wp + 16, 16))

    def fill(j, blocks, src, source_ids, target_ids, transpose):
        count = cnt_s[0, j]
        for k in range(SLOTS):
            rhs[pl.ds(k * BLK, BLK), :] = src[source_ids[k, 0, j]]
        for k in range(SLOTS):
            a = blocks[j, k]
            if transpose:
                wt[j, k] = a.T
            target = jnp.where(k < count, target_ids[k, 0, j], -1)
            for b in range(NB):
                lhs[pl.ds(b * BLK, BLK), pl.ds(k * BLK, BLK)] = jnp.where(
                    target == b, a, jnp.zeros_like(a)
                )

    def relay_forward(t):
        kappa, idx = t // 8, lax.rem(t, 8)
        other = jnp.logical_or(idx == 1, idx >= 5)
        hh = jnp.where(other, 1 - yh, yh)
        off = jnp.where(
            idx <= 1, 0,
            jnp.where(
                jnp.logical_or(idx == 2, idx == 5), 3,
                jnp.where(jnp.logical_or(idx == 3, idx == 6), 1, 2),
            ),
        )
        xs = lax.rem(x + off, 4)
        piece = rbuf.at[kappa, hh, xs]

        @pl.when(t > 0)
        def _():
            wait_bytes(piece, r_rz.at[t])

        @pl.when(jnp.logical_and(t > 0, t < 32))
        def _():
            copy_to(piece, rbuf.at[kappa + 1, hh, xs], s_rz.at[t], r_rz.at[t + 8], behind).start()

        @pl.when(t == 1)
        def _():
            for n, (target, at) in enumerate(((right, 5), (left, 6), (opposite, 7))):
                copy_to(
                    rbuf.at[0, 1 - yh, x], rbuf.at[0, 1 - yh, x], s_src.at[4 + n], r_rz.at[at], target
                ).start()

        cl = lax.rem(kappa, 2)
        for n in range(2):
            near_n = near(4 * hh + xs, 4 * n + x, 1 - lo)
            role_n = jnp.where(kappa == 2, near_n, kappa // 3)
            skip = jnp.logical_or(
                jnp.logical_and(kappa == 0, near_n == 0), jnp.logical_and(kappa == 4, near_n == 1)
            )

            @pl.when(jnp.logical_not(skip))
            def _(n=n, role_n=role_n):
                copy_to(
                    piece, xbuf.at[cl, hh, xs, share], s_y.at[n * 32 + lax.rem(t, 32)],
                    r_y.at[cl * 8 + hh * 4 + xs], dev(z, n, x, 1 - lo, role_n),
                ).start()

    def forward_panel(c):
        cl = jnp.where(c < 8, 1, 0)
        m = lax.rem(c, 8)
        hh = jnp.where(lax.rem(m, 2) == 0, yh, 1 - yh)
        n = m // 2
        xs = lax.rem(x + jnp.where(n == 0, 0, jnp.where(n == 1, 3, jnp.where(n == 2, 1, 2))), 4)
        wait_bytes(xbuf.at[cl, hh, xs, pl.ds(AR, 4 * RB)], r_y.at[cl * 8 + hh * 4 + xs])
        for b in range(NB):
            stage[b] = xbuf[cl, hh, xs, pl.ds(b * BLK, BLK), :]
        fill(block_of(cl, 4 * hh + xs), wv, stage, cols_s, rows_s, True)
        acc[...] += jnp.dot(lhs[...], rhs[...], preferred_element_type=F32)

    def got_z0(o, hh):
        wait_recv(zbuf.at[0, hh], r_z0[o])
        start(zbuf.at[0, hh], xbuf.at[1, hh, x, arows], r_z1[o], ahead, role_cond=far_role if o == 0 else None)
        comp_direct(o, hh, 0, zbuf.at[0, hh], far_role if o == 0 else None)

    def got_z1(o, hh):
        mine = xbuf.at[1, hh, x, arows]
        wait_recv(mine, r_z1[o])
        start(mine, zbuf.at[1, hh], r_z2[o], ahead)
        start(mine, mine, r_dir[1][o][0], right)
        start(mine, mine, r_dir[1][o][1], left)

    def got_z2(o, hh):
        wait_recv(zbuf.at[1, hh], r_z2[o])
        start(zbuf.at[1, hh], zbuf.at[0, hh], r_z0[o], mate, role_cond=near_role)
        comp_direct(o, hh, 1, zbuf.at[1, hh])
        own = near(4 * hh + x, w)
        xbuf[0, hh, x, arows, :] = zbuf[1 - own, hh]

    def pass_opposite(cl, o, hh):
        from_left, from_right = xbuf.at[cl, hh, xl], xbuf.at[cl, hh, xr]
        whole = cl == 0 and o == 0
        cond = inner if whole else None
        part_l, part_r = (arows, arows) if whole else (low, high)
        wait_recv(from_left.at[arows], r_dir[cl][o][0])
        start(from_left.at[part_l], from_left.at[part_l], r_opp[cl][o][0], right, cond=cond)
        wait_recv(from_right.at[arows], r_dir[cl][o][1])
        start(
            from_right.at[part_r], from_right.at[part_r], r_opp[cl][o][0 if whole else 1], left, cond=cond
        )

    def wait_opposite(cl, o, hh):
        if cl == 0 and o == 0:
            wait_recv(xbuf.at[cl, hh, xo, arows], r_opp[cl][o][0])
        else:
            wait_recv(xbuf.at[cl, hh, xo, low], r_opp[cl][o][0])
            wait_recv(xbuf.at[cl, hh, xo, high], r_opp[cl][o][1])

    def by_role(near_at, far_at):
        return jnp.where(near_role, near_at, far_at)

    events = [
        (-1, 15, lambda: got_z0(0, yh)),
        (7, 17, lambda: got_z0(1, 1 - yh)),
        (7, 19, lambda: got_z1(0, yh)),
        (11, 22, lambda: got_z1(1, 1 - yh)),
        (13, 24, lambda: got_z2(0, yh)),
        (16, 27, lambda: got_z2(1, 1 - yh)),
        (14, 28, lambda: pass_opposite(1, 0, yh)),
        (18, 31, lambda: pass_opposite(1, 1, 1 - yh)),
        (20, 33, lambda: pass_opposite(0, 0, yh)),
        (23, 36, lambda: pass_opposite(0, 1, 1 - yh)),
        (24, 35, lambda: wait_opposite(1, 0, yh)),
        (25, 36, lambda: wait_opposite(1, 1, 1 - yh)),
        (32, 43, lambda: wait_opposite(0, 0, yh)),
        (33, 44, lambda: wait_opposite(0, 1, 1 - yh)),
    ]
    compute_from = by_role(18, 29)

    def forward_step(t, carry):
        for near_at, far_at, what in events:
            pl.when(t == by_role(near_at, far_at))(what)

        @pl.when(t < 40)
        def _():
            relay_forward(t)

        c = t - compute_from

        @pl.when(jnp.logical_and(c >= 0, c < 16))
        def _():
            forward_panel(c)

        return carry

    lax.fori_loop(0, FWD_STEPS, forward_step, 0)

    mid_src[...] = acc[...].astype(BF16)
    r_mid, r_sc = recv_slot(4), recv_slot(4)
    peers = [lax.rem(r + n, 4) for n in range(1, 4)]
    for peer in peers:
        start(mid_src.at[pl.ds(pl.multiple_of(peer * QR, QR), QR)], mid_in.at[r], r_mid + r, (i, peer))
    own_rows = pl.ds(pl.multiple_of(r * QR, QR), QR)
    total = acc[own_rows, :]
    f_own = feat[own_rows, :]
    divisor = dcol[own_rows, :]
    preact = jnp.dot(f_own, wself[...], preferred_element_type=F32) + bias[...].astype(F32)
    load_cot.wait()
    for peer in peers:
        wait_recv(mid_in.at[peer], r_mid + peer)
        total = total + mid_in[peer].astype(F32)
    neighbours = (total / divisor).astype(BF16)
    preact = preact + jnp.dot(neighbours, wneigh[...], preferred_element_type=F32)
    sig = jax.nn.sigmoid(preact)
    slope = sig * (1.0 + preact * (1.0 - sig))
    pre_grad = (cot[...].astype(F32) * slope).astype(BF16)
    contract = (((1,), (1,)), ((), ()))
    scaled = lax.dot_general(pre_grad, wneigh[...], contract, preferred_element_type=F32)
    sbuf[own_rows, :] = (scaled / divisor).astype(BF16)
    for peer in peers:
        start(sbuf.at[own_rows], sbuf.at[own_rows], r_sc + r, (i, peer))
    out[...] = (preact * sig).astype(BF16)
    base[...] = lax.dot_general(pre_grad, wself[...], contract, preferred_element_type=F32)
    for peer in peers:
        wait_recv(sbuf.at[pl.ds(pl.multiple_of(peer * QR, QR), QR)], r_sc + peer)
    for b in range(NB):
        sstage[b] = sbuf[pl.ds(b * BLK, BLK), :]

    b_opp = [[recv_slot(2) for o in range(2)] for cl in range(2)]
    b_dir = [[[recv_slot() for _ in range(2)] for _ in order] for _ in range(2)]
    b_chain = [[recv_slot() for _ in order] for _ in range(3)]
    r_fa = recv_slot(4)
    mine = 2 * lo + yh
    far_opp_side = jnp.where(x <= 1, 0, 1)
    far_opp_to = dev(z, yh, jnp.where(x <= 1, xr, xl), lo, role)

    def backward_panel(c):
        cl = jnp.where(c < 8, 0, 1)
        m = lax.rem(c, 8)
        hh, n = lax.rem(m, 2), m // 2
        xs = lax.rem(x + jnp.where(n == 0, 2, jnp.where(n == 1, 3, jnp.where(n == 2, 1, 0))), 4)
        fill(block_of(cl, 4 * hh + xs), wt, sstage, rows_s, cols_s, False)
        pbuf[cl, hh, xs] = jnp.dot(lhs[...], rhs[...], preferred_element_type=F32).astype(BF16)
        at = cl * 8 + hh * 4 + xs
        for q in range(4):
            copy_to(
                pbuf.at[cl, hh, xs, pl.ds(AR + RB * q, RB)], rin.at[yh, role, cl, hh, xs],
                s_p.at[at * 4 + q], r_p.at[(yh * 2 + role) * 16 + at],
                dev(z, q // 2, x, 1 - lo, q % 2),
            ).start()

    def relay_backward(u):
        kappa, idx = 4 - u // 8, lax.rem(u, 8)
        hh, n = lax.rem(idx, 2), idx // 2
        xs = lax.rem(x + jnp.where(n == 0, 2, jnp.where(n == 1, 3, jnp.where(n == 2, 1, 0))), 4)
        cl = lax.rem(kappa, 2)
        tacc[...] = jnp.zeros_like(tacc)
        for n in range(2):
            near_n = near(4 * hh + xs, 4 * n + x, 1 - lo)
            role_n = jnp.where(kappa == 2, near_n, kappa // 3)
            skip = jnp.logical_or(
                jnp.logical_and(kappa == 0, near_n == 0), jnp.logical_and(kappa == 4, near_n == 1)
            )

            @pl.when(jnp.logical_not(skip))
            def _(n=n, role_n=role_n):
                wait_bytes(
                    rin.at[n, role_n, cl, hh, xs], r_p.at[(n * 2 + role_n) * 16 + cl * 8 + hh * 4 + xs]
                )
                tacc[...] += rin[n, role_n, cl, hh, xs].astype(F32)

        @pl.when(u >= 8)
        def _():
            wait_bytes(tin.at[kappa, hh, xs], r_t.at[u - 8])
            tacc[...] += tin[kappa, hh, xs].astype(F32)

        tout[kappa, hh, xs] = tacc[...].astype(BF16)

        @pl.when(u < 32)
        def _():
            copy_to(tout.at[kappa, hh, xs], tin.at[kappa - 1, hh, xs], s_t.at[u], r_t.at[u], ahead).start()

        @pl.when(u >= 32)
        def _():
            final_relay(idx, hh, xs, True)

    def final_relay(idx, hh, xs, begin):
        source = lo * 4 + x
        for q in range(4):
            for part, (a, rows, quarter, at) in enumerate(B_PARTS[q]):
                here = jnp.logical_and(
                    jnp.logical_and(hh == yh, xs == x), jnp.logical_and(r == quarter, relay == q)
                )
                gone = jnp.logical_and(relay == q, jnp.logical_not(here))
                src, dst = tout.at[0, hh, xs, pl.ds(a, rows)], fin_b.at[source, pl.ds(at, rows)]
                send_sem = s_fb.at[idx * 2 + part]
                if begin:
                    @pl.when(gone)
                    def _(src=src, dst=dst, send_sem=send_sem, quarter=quarter):
                        copy_to(
                            src, dst, send_sem, r_fb.at[source], (z * 8 + hh * 4 + xs, quarter)
                        ).start()

                    @pl.when(here)
                    def _(src=src, dst=dst):
                        pltpu.make_async_copy(src, dst, r_fb.at[source]).start()
                else:
                    @pl.when(gone)
                    def _(src=src, send_sem=send_sem):
                        wait_bytes(src, send_sem)

    def send_opposite(cl):
        for o, hh in enumerate(order):
            if cl == 0 and o == 0:
                start(
                    pbuf.at[cl, hh, xo, arows], opp_in.at[cl, o, far_opp_side],
                    b_opp[cl][o] + far_opp_side, far_opp_to,
                )
            else:
                start(pbuf.at[cl, hh, xo, low], opp_in.at[cl, o, 1, low], b_opp[cl][o] + 1, left)
                start(pbuf.at[cl, hh, xo, high], opp_in.at[cl, o, 0, high], b_opp[cl][o], right)

    def send_direct(cl):
        for o, hh in enumerate(order):
            def merge(side, xs, part, o=o, hh=hh):
                wait_recv(opp_in.at[cl, o, side, part], b_opp[cl][o] + side)
                pbuf[cl, hh, xs, part, :] = (
                    pbuf[cl, hh, xs, part, :].astype(F32) + opp_in[cl, o, side, part, :].astype(F32)
                ).astype(BF16)

            if cl == 0 and o == 0:
                @pl.when(inner)
                def _(merge=merge):
                    merge(0, xr, arows)
                    merge(1, xl, arows)
            else:
                merge(0, xr, high)
                merge(1, xl, low)
            start(pbuf.at[cl, hh, xl, arows], dir_in.at[cl, o, 1], b_dir[cl][o][1], left)
            start(pbuf.at[cl, hh, xr, arows], dir_in.at[cl, o, 0], b_dir[cl][o][0], right)

    def sum_composite(o, hh):
        wait_recv(dir_in.at[0, o, 0], b_dir[0][o][0])
        wait_recv(dir_in.at[0, o, 1], b_dir[0][o][1])
        wp = 4 * hh + x
        n_own = near(wp, w).astype(F32)
        n_left = near(wp, 4 * yh + xl).astype(F32)
        n_right = near(wp, 4 * yh + xr).astype(F32)
        v_own = pbuf[0, hh, x, arows, :].astype(F32)
        v_left = dir_in[0, o, 0].astype(F32)
        v_right = dir_in[0, o, 1].astype(F32)
        znear[o] = n_own * v_own + n_left * v_left + n_right * v_right
        zfar[o] = (1.0 - n_own) * v_own + (1.0 - n_left) * v_left + (1.0 - n_right) * v_right

    def chain_two(o):
        @pl.when(far_role)
        def _():
            chain_out[2, o] = zfar[o].astype(BF16)

        @pl.when(near_role)
        def _():
            wait_recv(chain_in.at[2, o], b_chain[2][o])
            chain_out[2, o] = (zfar[o] + chain_in[2, o].astype(F32)).astype(BF16)

        start(chain_out.at[2, o], chain_in.at[1, o], b_chain[1][o], behind)

    def sum_whole(o, hh):
        wait_recv(dir_in.at[1, o, 0], b_dir[1][o][0])
        wait_recv(dir_in.at[1, o, 1], b_dir[1][o][1])
        zone[o] = (
            pbuf[1, hh, x, arows, :].astype(F32) + dir_in[1, o, 0].astype(F32) + dir_in[1, o, 1].astype(F32)
        )

    def chain_one(o):
        wait_recv(chain_in.at[1, o], b_chain[1][o])
        chain_out[1, o] = (zone[o] + chain_in[1, o].astype(F32)).astype(BF16)
        start(chain_out.at[1, o], chain_in.at[0, o], b_chain[0][o], behind)

    def chain_zero(o, hh):
        wait_recv(chain_in.at[0, o], b_chain[0][o])
        chain_out[0, o] = (znear[o] + chain_in[0, o].astype(F32)).astype(BF16)
        start(chain_out.at[0, o], chain_in.at[2, o], b_chain[2][o], mate, role_cond=far_role)
        for a, rows, quarter, at in A_PARTS:
            src, dst = chain_out.at[0, o, pl.ds(a, rows)], fin_a.at[mine, pl.ds(at, rows)]
            cond = None
            if o == 0:
                cond = not_quarter[quarter]

                @pl.when(jnp.logical_and(near_role, r == quarter))
                def _(src=src, dst=dst):
                    pltpu.make_async_copy(src, dst, recv_sems.at[r_fa + mine]).start()
            start(
                src, dst, r_fa + mine, (z * 8 + hh * 4 + x, quarter), cond=cond, role_cond=near_role
            )

    late = by_role(BWD_LATE, 0)
    back_events = [
        (BWD_LATE + 2, 2, lambda: send_opposite(0)),
        (BWD_LATE + 6, 6, lambda: send_direct(0)),
        (BWD_LATE + 10, 10, lambda: send_opposite(1)),
        (BWD_LATE + 14, 14, lambda: send_direct(1)),
        (BWD_LATE + 13, 12, lambda: sum_composite(0, yh)),
        (BWD_LATE + 15, 13, lambda: sum_composite(1, 1 - yh)),
        (27, 12, lambda: chain_two(0)),
        (29, 13, lambda: chain_two(1)),
        (32, 20, lambda: sum_whole(0, yh)),
        (34, 22, lambda: sum_whole(1, 1 - yh)),
        (32, 20, lambda: chain_one(0)),
        (34, 22, lambda: chain_one(1)),
        (38, 25, lambda: chain_zero(0, yh)),
        (40, 27, lambda: chain_zero(1, 1 - yh)),
    ]

    def backward_step(t, carry):
        for near_at, far_at, what in back_events:
            pl.when(t == by_role(near_at, far_at))(what)

        c = t - late

        @pl.when(jnp.logical_and(c >= 0, c < 16))
        def _():
            backward_panel(c)

        u = t - 2

        @pl.when(jnp.logical_and(u >= 0, u < 40))
        def _():
            relay_backward(u)

        return carry

    lax.fori_loop(0, BWD_STEPS, backward_step, 0)

    for quarter in range(4):
        a_rows = sum(p[1] for p in A_PARTS if p[2] == quarter)

        @pl.when(r == quarter)
        def _(a_rows=a_rows):
            if a_rows:
                part = pl.ds(0, a_rows)
                for source in range(4):
                    wait_recv(fin_a.at[source, part], r_fa + source)
                result = base[part, :]
                for source in range(4):
                    result = result + fin_a[source, part, :].astype(F32)
                grad[part, :] = result.astype(BF16)
            if a_rows < QR:
                part = pl.ds(a_rows, QR - a_rows)
                for source in range(8):
                    wait_bytes(fin_b.at[source, part], r_fb.at[source])
                result = base[part, :]
                for source in range(8):
                    result = result + fin_b[source, part, :].astype(F32)
                grad[part, :] = result.astype(BF16)

    drain()
    drain_many(s_rz, 32, RB)
    drain_many(s_src, 7, RB)
    drain_many(s_y, 64, RB)
    drain_many(s_p, 64, RB)
    drain_many(s_t, 32, RB)

    def drain_final(idx, carry):
        hh, n = lax.rem(idx, 2), idx // 2
        xs = lax.rem(x + jnp.where(n == 0, 2, jnp.where(n == 1, 3, jnp.where(n == 2, 1, 0))), 4)
        final_relay(idx, hh, xs, False)
        return carry

    lax.fori_loop(0, 8, drain_final, 0)


def on_device(
    features, degrees, cotangent, self_weight, neigh_weight, bias_vector,
    block_values, block_rows, block_cols, block_count,
):
    vmem = pl.BlockSpec(memory_space=pltpu.VMEM)
    smem = pl.BlockSpec(memory_space=pltpu.SMEM)
    anyspace = pl.BlockSpec(memory_space=pl.ANY)
    panel = (PR, HID)
    apanel = (AR, HID)
    piece = (RB, HID)
    dma = pltpu.SemaphoreType.DMA
    return pl.pallas_call(
        kernel,
        out_shape=(
            jax.ShapeDtypeStruct((QR, HID), BF16),
            jax.ShapeDtypeStruct((QR, HID), BF16),
        ),
        in_specs=[smem, smem, smem, vmem, vmem, anyspace, vmem, vmem, vmem, anyspace],
        out_specs=(vmem, vmem),
        scratch_shapes=[
            pltpu.VMEM((16, SLOTS, BLK, BLK), BF16),
            pltpu.VMEM((16, SLOTS, BLK, BLK), BF16),
            pltpu.VMEM((2, 2, 4) + panel, BF16),
            pltpu.VMEM((2, 2) + apanel, BF16),
            pltpu.VMEM(panel, F32),
            pltpu.VMEM((PR, SLOTS * BLK), BF16),
            pltpu.VMEM((SLOTS * BLK, HID), BF16),
            pltpu.VMEM((NB, BLK, HID), BF16),
            pltpu.VMEM((NB, BLK, HID), BF16),
            pltpu.VMEM((QR, HID), BF16),
            pltpu.VMEM(panel, F32),
            pltpu.VMEM(panel, BF16),
            pltpu.VMEM((4, QR, HID), BF16),
            pltpu.VMEM(panel, BF16),
            pltpu.VMEM((QR, HID), F32),
            pltpu.VMEM((5, 2, 4) + piece, BF16),
            pltpu.VMEM((2, 2, 4) + panel, BF16),
            pltpu.VMEM((2, 2, 2) + apanel, BF16),
            pltpu.VMEM((2, 2, 2) + apanel, BF16),
            pltpu.VMEM((2,) + apanel, F32),
            pltpu.VMEM((2,) + apanel, F32),
            pltpu.VMEM((2,) + apanel, F32),
            pltpu.VMEM((3, 2) + apanel, BF16),
            pltpu.VMEM((3, 2) + apanel, BF16),
            pltpu.VMEM((4, QR, HID), BF16),
            pltpu.VMEM((2, 2, 2, 2, 4) + piece, BF16),
            pltpu.VMEM((4, 2, 4) + piece, BF16),
            pltpu.VMEM((5, 2, 4) + piece, BF16),
            pltpu.VMEM(piece, F32),
            pltpu.VMEM((8, QR, HID), BF16),
            dma((80,)),
            dma((80,)),
            dma((2,)),
            pltpu.SemaphoreType.REGULAR,
            dma((32,)),
            dma((40,)),
            dma((7,)),
            dma((64,)),
            dma((16,)),
            dma((64,)),
            dma((64,)),
            dma((32,)),
            dma((32,)),
            dma((16,)),
            dma((8,)),
        ],
        compiler_params=pltpu.CompilerParams(
            collective_id=0, has_side_effects=True, vmem_limit_bytes=60 * 1024 * 1024
        ),
        name="sage_layer",
    )(
        jnp.transpose(block_rows, (2, 0, 1)), jnp.transpose(block_cols, (2, 0, 1)), block_count,
        features, degrees.reshape(NB, BLK), cotangent,
        self_weight, neigh_weight, bias_vector[None, :], block_values,
    )


def solution(mesh):
    return jax.shard_map(
        on_device,
        mesh=mesh,
        in_specs=(
            P("rows", None),
            P("rows"),
            P("rows", None),
            P(),
            P(),
            P(),
            P("rows", "rep", None, None, None),
            P("rows", "rep", None),
            P("rows", "rep", None),
            P("rows", "rep"),
        ),
        out_specs=(P(("rows", "rep"), None), P(("rows", "rep"), None)),
        check_vma=False,
    )
```

```python
import jax
import jax.numpy as jnp
from jax import lax
from jax.experimental import pallas as pl
from jax.experimental.pallas import tpu as pltpu
from jax.sharding import PartitionSpec as P

MESH = pl.DeviceIdType.MESH
F32 = jnp.float32
BF16 = jnp.bfloat16
NB = 6
BLK = 128
SLOTS = 12
PR = NB * BLK
HID = 256
QR = PR // 4
RB = 80
AR = PR - 4 * RB
HA = AR // 2
FWD_STEPS = 47
BUILD_FROM = 3
BWD_STEPS = 48


def quarter_parts(start, size):
    parts = []
    for quarter in range(4):
        a, b = max(start, quarter * QR), min(start + size, (quarter + 1) * QR)
        if a < b:
            parts.append((a - start, b - a, quarter, a - quarter * QR))
    return parts


A_PARTS = quarter_parts(0, AR)
B_PARTS = [quarter_parts(AR + q * RB, RB) for q in range(4)]


def kernel(
    rows_s, cols_s, cnt_s, feat, deg, cot_hbm, wself, wneigh, bias, w_hbm,
    both,
    wv, dense, merged, xbuf, zbuf, acc, cot, dcol,
    mid_src, mid_in, sbuf, sflip, base, rbuf,
    pbuf, opp_in, dir_in, znear, zfar, zone, chain_in, chain_out, fin_a,
    rin, tin, tout, tacc, fin_b,
    send_sems, recv_sems, load_sems, go_sem,
    s_rz, r_rz, s_src, s_y, r_y, s_p, r_p, s_t, r_t, s_fb, r_fb,
):
    i = lax.axis_index("rows")
    r = lax.axis_index("rep")
    z, yh, x, w = i // 8, lax.rem(i // 4, 2), lax.rem(i, 4), lax.rem(i, 8)
    lo, core = r // 2, lax.rem(r, 2)
    role = lax.rem(core + lo, 2)
    step = 1 - 2 * lo
    znext, zprev = lax.rem(z + step + 8, 8), lax.rem(z - step + 8, 8)
    xr, xl, xo = lax.rem(x + 1, 4), lax.rem(x + 3, 4), lax.rem(x + 2, 4)
    inner = jnp.logical_or(x == 1, x == 2)
    near_role, far_role = role == 0, role == 1
    relay = 2 * yh + role
    share = pl.ds(pl.multiple_of(AR + RB * relay, 16), RB)
    share_across = pl.ds(pl.multiple_of(AR + RB * (2 * (1 - yh) + role), 16), RB)

    def dev(z_, yh_, x_, lo_, role_):
        return (z_ * 8 + yh_ * 4 + x_, 2 * lo_ + lax.rem(role_ + lo_, 2))

    left, right = dev(z, yh, xl, lo, role), dev(z, yh, xr, lo, role)
    opposite = dev(z, yh, xo, lo, role)
    ahead, behind = dev(znext, yh, x, lo, role), dev(zprev, yh, x, lo, role)
    mate = dev(z, yh, x, lo, 1 - role)
    across = dev(z, 1 - yh, x, 1 - lo, role)

    def near(wp, w_at, lo_at=lo):
        return lax.rem(jnp.where(wp <= w_at, 1, 0) + lo_at, 2)

    load_w = pltpu.make_async_copy(w_hbm.at[0], wv, load_sems.at[0])
    load_w.start()
    load_cot = pltpu.make_async_copy(cot_hbm.at[pl.ds(r * QR, QR)], cot, load_sems.at[1])
    load_cot.start()

    barrier = pltpu.get_barrier_semaphore()

    def greet(n, carry):
        at = lax.rem(w * 4 + r + n, 32)
        pl.semaphore_signal(
            barrier, inc=1, device_id=(z * 8 + at // 4, lax.rem(at, 4)), device_id_type=MESH
        )
        return carry

    lax.fori_loop(1, 32, greet, 0)
    pl.semaphore_signal(barrier, inc=1, device_id=ahead, device_id_type=MESH)
    pl.semaphore_signal(barrier, inc=1, device_id=behind, device_id_type=MESH)
    pl.semaphore_wait(barrier, 33)

    sends, recvs, pending = [0], [0], []

    def recv_slot(n=1):
        recvs[0] += n
        return recvs[0] - n

    def copy_to(src, dst, send_sem, recv_sem, device):
        return pltpu.make_async_remote_copy(
            src_ref=src, dst_ref=dst, send_sem=send_sem, recv_sem=recv_sem,
            device_id=device, device_id_type=MESH,
        )

    def joined(cond, role_cond):
        if cond is None or role_cond is None:
            return role_cond if cond is None else cond
        return jnp.logical_and(cond, role_cond)

    def start(src, dst, slot, device, cond=None, role_cond=None, send_slot=None):
        if send_slot is None:
            send_slot = sends[0]
            sends[0] += 1
        copy = copy_to(src, dst, send_sems.at[send_slot], recv_sems.at[slot], device)
        both = joined(cond, role_cond)
        if both is None:
            copy.start()
        else:
            pl.when(both)(lambda: copy.start())
        pending.append((cond, role_cond, src.shape[-2], send_slot))
        return send_slot

    def wait_bytes(ref, sem):
        pltpu.make_async_copy(ref, ref, sem).wait()

    def wait_recv(ref, slot):
        wait_bytes(ref, recv_sems.at[slot])

    def drain():
        for cond, role_cond, rows, slot in pending:
            cond = joined(cond, role_cond)

            def wait(rows=rows, slot=slot):
                wait_bytes(zbuf.at[0, 0, pl.ds(0, rows)], send_sems.at[slot])

            if cond is None:
                wait()
            else:
                pl.when(cond)(wait)
        pending.clear()

    def drain_many(sems, count, rows):
        def wait(n, carry):
            wait_bytes(zbuf.at[0, 0, pl.ds(0, rows)], sems.at[n])
            return carry

        lax.fori_loop(0, count, wait, 0)

    order = (yh, 1 - yh)
    arows = pl.ds(0, AR)
    low, high = pl.ds(0, HA), pl.ds(HA, HA)

    not_quarter = [r != quarter for quarter in range(4)]
    near_side = [
        [near(4 * hh + x, 4 * yh + nx) == 1 for nx in (xr, xl)] for hh in order
    ]
    far_side = [
        [near(4 * hh + x, 4 * yh + nx) == 0 for nx in (xr, xl)] for hh in order
    ]

    halves = (low, high)

    def slots_for(*counts):
        if not counts:
            return recv_slot()
        return [slots_for(*counts[1:]) for _ in range(counts[0])]

    r_z0, r_z1, r_z2 = slots_for(2, 2), slots_for(2, 2), slots_for(2, 2)
    r_dir = slots_for(2, 2, 2, 2)
    r_opp = slots_for(2, 2, 2)
    comp_slots = [[[None, None], [None, None]], [[None, None], [None, None]]]

    def comp_direct(o, s, hh, idx, src, role_cond=None):
        flags = near_side if idx == 0 else far_side
        for side, target in enumerate((right, left)):
            comp_slots[o][s][side] = start(
                src, xbuf.at[0, hh, x, halves[s]], r_dir[0][o][s][side], target,
                cond=flags[o][side], role_cond=role_cond, send_slot=comp_slots[o][s][side],
            )

    own_b = feat.at[share]
    copy_to(own_b, rbuf.at[1, yh, x], s_rz.at[0], r_rz.at[8], behind).start()
    copy_to(feat.at[share_across], rbuf.at[0, yh, x], s_src.at[0], r_rz.at[1], across).start()
    for n, (target, at) in enumerate(((right, 2), (left, 3), (opposite, 4))):
        copy_to(own_b, rbuf.at[0, yh, x], s_src.at[1 + n], r_rz.at[at], target).start()
    for s, half in enumerate(halves):
        start(feat.at[half], xbuf.at[1, yh, x, half], r_z1[0][s], ahead, role_cond=near_role)
    for s, half in enumerate(halves):
        start(feat.at[half], zbuf.at[0, yh, half], r_z0[1][s], across, role_cond=near_role)
    for s, half in enumerate(halves):
        comp_direct(0, s, yh, 0, feat.at[half], near_role)

    @pl.when(near_role)
    def _():
        zbuf[0, yh] = feat[arows, :]

    rbuf[0, yh, x] = feat[share, :]

    dcol_rows = deg[...].astype(F32)
    dcol_t = jnp.concatenate([dcol_rows, dcol_rows[0:2]], axis=0).T
    for b in range(NB):
        dcol[pl.ds(b * BLK, BLK), :] = jnp.broadcast_to(dcol_t[:, b : b + 1], (BLK, HID))

    acc[...] = jnp.zeros_like(acc)
    merged[SLOTS] = jnp.zeros((BLK, BLK), BF16)

    def block_of(cl, wp):
        return jnp.where(cl == 1, 8 + w - wp, lax.rem(w - wp + 16, 16))

    def build(c):
        cl, hh, xs = forward_place(c)
        wp = 4 * hh + xs
        j = block_of(cl, wp)
        count = cnt_s[0, j]
        places = [
            jnp.where(k < count, rows_s[k, 0, j] * NB + cols_s[k, 0, j], -1) for k in range(SLOTS)
        ]
        for k in range(SLOTS):
            before = SLOTS
            for earlier in range(k):
                before = jnp.where(places[earlier] == places[k], earlier, before)
            merged[k] = wv[j, k] if k == 0 else wv[j, k] + merged[before]
        for b in range(NB):
            for a in range(NB):
                last = SLOTS
                for k in range(SLOTS):
                    last = jnp.where(places[k] == b * NB + a, k, last)
                dense[cl * 8 + wp, pl.ds(b * BLK, BLK), pl.ds(a * BLK, BLK)] = merged[last]

    def forward_place(c):
        cl = jnp.where(c < 8, 1, 0)
        m = lax.rem(c, 8)
        hh = jnp.where(lax.rem(m, 2) == 0, yh, 1 - yh)
        n = m // 2
        xs = lax.rem(x + jnp.where(n == 0, 0, jnp.where(n == 1, 3, jnp.where(n == 2, 1, 2))), 4)
        return cl, hh, xs

    def relay_forward(t):
        kappa, idx = t // 8, lax.rem(t, 8)
        other = jnp.logical_or(idx == 1, idx >= 5)
        hh = jnp.where(other, 1 - yh, yh)
        off = jnp.where(
            idx <= 1, 0,
            jnp.where(
                jnp.logical_or(idx == 2, idx == 5), 3,
                jnp.where(jnp.logical_or(idx == 3, idx == 6), 1, 2),
            ),
        )
        xs = lax.rem(x + off, 4)
        piece = rbuf.at[kappa, hh, xs]

        @pl.when(t > 0)
        def _():
            wait_bytes(piece, r_rz.at[t])

        @pl.when(jnp.logical_and(t > 0, t < 32))
        def _():
            copy_to(piece, rbuf.at[kappa + 1, hh, xs], s_rz.at[t], r_rz.at[t + 8], behind).start()

        @pl.when(t == 1)
        def _():
            for n, (target, at) in enumerate(((right, 5), (left, 6), (opposite, 7))):
                copy_to(
                    rbuf.at[0, 1 - yh, x], rbuf.at[0, 1 - yh, x], s_src.at[4 + n], r_rz.at[at], target
                ).start()

        cl = lax.rem(kappa, 2)
        for n in range(2):
            near_n = near(4 * hh + xs, 4 * n + x, 1 - lo)
            role_n = jnp.where(kappa == 2, near_n, kappa // 3)
            skip = jnp.logical_or(
                jnp.logical_and(kappa == 0, near_n == 0), jnp.logical_and(kappa == 4, near_n == 1)
            )

            @pl.when(jnp.logical_not(skip))
            def _(n=n, role_n=role_n):
                copy_to(
                    piece, xbuf.at[cl, hh, xs, share], s_y.at[n * 32 + lax.rem(t, 32)],
                    r_y.at[cl * 8 + hh * 4 + xs], dev(z, n, x, 1 - lo, role_n),
                ).start()

    def forward_panel(c):
        cl, hh, xs = forward_place(c)
        at = cl * 8 + hh * 4 + xs
        wait_bytes(xbuf.at[cl, hh, xs, pl.ds(AR, 4 * RB)], r_y.at[at])
        acc[...] += jnp.dot(dense[at], xbuf[cl, hh, xs], preferred_element_type=F32)

    def got_z0(o, s, hh):
        piece = zbuf.at[0, hh, halves[s]]
        role_cond = far_role if o == 0 else None
        wait_recv(piece, r_z0[o][s])
        start(piece, xbuf.at[1, hh, x, halves[s]], r_z1[o][s], ahead, role_cond=role_cond)
        comp_direct(o, s, hh, 0, piece, role_cond)

    def got_z1(o, s, hh):
        piece = xbuf.at[1, hh, x, halves[s]]
        wait_recv(piece, r_z1[o][s])
        start(piece, zbuf.at[1, hh, halves[s]], r_z2[o][s], ahead)
        start(piece, piece, r_dir[1][o][s][0], right)
        start(piece, piece, r_dir[1][o][s][1], left)

    def got_z2(o, s, hh):
        piece = zbuf.at[1, hh, halves[s]]
        wait_recv(piece, r_z2[o][s])
        start(piece, zbuf.at[0, hh, halves[s]], r_z0[o][s], mate, role_cond=near_role)
        comp_direct(o, s, hh, 1, piece)
        own = near(4 * hh + x, w)
        xbuf[0, hh, x, halves[s], :] = zbuf[1 - own, hh, halves[s], :]

    def pass_opposite(cl, o, s, hh):
        whole = cl == 0 and o == 0
        cond = inner if whole else None
        for side, (xs, target) in enumerate(((xl, right), (xr, left))):
            piece = xbuf.at[cl, hh, xs, halves[s]]
            wait_recv(piece, r_dir[cl][o][s][side])
            if whole or s == side:
                start(piece, piece, r_opp[cl][o][s], target, cond=cond)

    def wait_opposite(cl, o, s, hh):
        wait_recv(xbuf.at[cl, hh, xo, halves[s]], r_opp[cl][o][s])

    def by_role(near_at, far_at):
        return jnp.where(near_role, near_at, far_at)

    events = [
        (-1, 12, lambda: got_z0(0, 0, order[0])),
        (38, 43, lambda: wait_opposite(0, 1, 1, order[1])),
        (4, 15, lambda: got_z0(1, 0, order[1])),
        (4, 17, lambda: got_z0(1, 1, order[1])),
        (4, 18, lambda: got_z1(0, 0, order[0])),
        (25, 36, lambda: pass_opposite(0, 1, 1, order[1])),
        (7, 23, lambda: got_z1(1, 0, order[1])),
        (14, 27, lambda: got_z2(1, 0, order[1])),
        (11, 24, lambda: got_z2(0, 0, order[0])),
        (11, 24, lambda: got_z2(0, 1, order[0])),
        (9, 23, lambda: got_z1(1, 1, order[1])),
        (16, 30, lambda: got_z2(1, 1, order[1])),
        (12, 28, lambda: pass_opposite(1, 0, 0, order[0])),
        (13, 30, lambda: pass_opposite(1, 0, 1, order[0])),
        (4, 21, lambda: got_z1(0, 1, order[0])),
        (17, 32, lambda: pass_opposite(1, 1, 1, order[1])),
        (29, 37, lambda: wait_opposite(1, 1, 0, order[1])),
        (16, 30, lambda: pass_opposite(1, 1, 0, order[1])),
        (24, 39, lambda: pass_opposite(0, 1, 0, order[1])),
        (19, 35, lambda: pass_opposite(0, 0, 1, order[0])),
        (23, 36, lambda: wait_opposite(1, 0, 1, order[0])),
        (24, 35, lambda: wait_opposite(1, 0, 0, order[0])),
        (28, 33, lambda: pass_opposite(0, 0, 0, order[0])),
        (26, 37, lambda: wait_opposite(1, 1, 1, order[1])),
        (35, 39, lambda: wait_opposite(0, 0, 0, order[0])),
        (-1, 14, lambda: got_z0(0, 1, order[0])),
        (32, 45, lambda: wait_opposite(0, 1, 0, order[1])),
        (30, 40, lambda: wait_opposite(0, 0, 1, order[0])),
    ]
    compute_from = by_role(24, 31)

    def forward_step(t, carry):
        for near_at, far_at, what in events:
            pl.when(t == by_role(near_at, far_at))(what)

        @pl.when(t < 40)
        def _():
            relay_forward(t)

        @pl.when(t == BUILD_FROM)
        def _():
            load_w.wait()

        @pl.when(jnp.logical_and(t >= BUILD_FROM, t < BUILD_FROM + 16))
        def _():
            build(t - BUILD_FROM)

        c = t - compute_from

        @pl.when(jnp.logical_and(c >= 0, c < 16))
        def _():
            forward_panel(c)

        return carry

    lax.fori_loop(0, FWD_STEPS, forward_step, 0)

    mid_src[...] = acc[...].astype(BF16)
    r_mid, r_sc = recv_slot(4), recv_slot(4)
    peers = [lax.rem(r + n, 4) for n in range(1, 4)]
    for peer in peers:
        start(mid_src.at[pl.ds(pl.multiple_of(peer * QR, QR), QR)], mid_in.at[r], r_mid + r, (i, peer))
    own_rows = pl.ds(pl.multiple_of(r * QR, QR), QR)
    total = acc[own_rows, :]
    f_own = feat[own_rows, :]
    divisor = dcol[own_rows, :]
    preact = jnp.dot(f_own, wself[...], preferred_element_type=F32) + bias[...].astype(F32)[None, :]
    load_cot.wait()
    for peer in peers:
        wait_recv(mid_in.at[peer], r_mid + peer)
        total = total + mid_in[peer].astype(F32)
    neighbours = (total / divisor).astype(BF16)
    preact = preact + jnp.dot(neighbours, wneigh[...], preferred_element_type=F32)
    sig = jax.nn.sigmoid(preact)
    slope = sig * (1.0 + preact * (1.0 - sig))
    pre_grad = (cot[...].astype(F32) * slope).astype(BF16)
    contract = (((1,), (1,)), ((), ()))
    scaled = lax.dot_general(pre_grad, wneigh[...], contract, preferred_element_type=F32)
    sbuf[own_rows, :] = (scaled / divisor).astype(BF16)
    for peer in peers:
        start(sbuf.at[own_rows], sbuf.at[own_rows], r_sc + r, (i, peer))
    both[:, 0:HID] = (preact * sig).astype(BF16)
    base[...] = lax.dot_general(pre_grad, wself[...], contract, preferred_element_type=F32)
    for peer in peers:
        wait_recv(sbuf.at[pl.ds(pl.multiple_of(peer * QR, QR), QR)], r_sc + peer)
    sflip[...] = sbuf[...].T

    b_opp = [[recv_slot(2) for o in range(2)] for cl in range(2)]
    b_dir = [[[recv_slot() for _ in range(2)] for _ in order] for _ in range(2)]
    b_chain = [[recv_slot() for _ in order] for _ in range(3)]
    r_fa = recv_slot(4)
    mine = 2 * lo + yh
    far_opp_side = jnp.where(x <= 1, 0, 1)
    far_opp_to = dev(z, yh, jnp.where(x <= 1, xr, xl), lo, role)

    def backward_panel(c):
        cl = jnp.where(c < 8, 0, 1)
        m = lax.rem(c, 8)
        hh, n = lax.rem(m, 2), m // 2
        xs = lax.rem(x + jnp.where(n == 0, 2, jnp.where(n == 1, 3, jnp.where(n == 2, 1, 0))), 4)
        at = cl * 8 + hh * 4 + xs
        flipped = jnp.dot(sflip[...], dense[at], preferred_element_type=F32)
        pbuf[cl, hh, xs] = flipped.astype(BF16).T
        for q in range(4):
            copy_to(
                pbuf.at[cl, hh, xs, pl.ds(AR + RB * q, RB)], rin.at[yh, role, cl, hh, xs],
                s_p.at[at * 4 + q], r_p.at[(yh * 2 + role) * 16 + at],
                dev(z, q // 2, x, 1 - lo, q % 2),
            ).start()

    def relay_backward(u):
        kappa, idx = 4 - u // 8, lax.rem(u, 8)
        hh, n = lax.rem(idx, 2), idx // 2
        xs = lax.rem(x + jnp.where(n == 0, 2, jnp.where(n == 1, 3, jnp.where(n == 2, 1, 0))), 4)
        cl = lax.rem(kappa, 2)
        tacc[...] = jnp.zeros_like(tacc)
        for n in range(2):
            near_n = near(4 * hh + xs, 4 * n + x, 1 - lo)
            role_n = jnp.where(kappa == 2, near_n, kappa // 3)
            skip = jnp.logical_or(
                jnp.logical_and(kappa == 0, near_n == 0), jnp.logical_and(kappa == 4, near_n == 1)
            )

            @pl.when(jnp.logical_not(skip))
            def _(n=n, role_n=role_n):
                wait_bytes(
                    rin.at[n, role_n, cl, hh, xs], r_p.at[(n * 2 + role_n) * 16 + cl * 8 + hh * 4 + xs]
                )
                tacc[...] += rin[n, role_n, cl, hh, xs].astype(F32)

        @pl.when(u >= 8)
        def _():
            wait_bytes(tin.at[kappa, hh, xs], r_t.at[u - 8])
            tacc[...] += tin[kappa, hh, xs].astype(F32)

        tout[kappa, hh, xs] = tacc[...].astype(BF16)

        @pl.when(u < 32)
        def _():
            copy_to(tout.at[kappa, hh, xs], tin.at[kappa - 1, hh, xs], s_t.at[u], r_t.at[u], ahead).start()

        @pl.when(u >= 32)
        def _():
            final_relay(idx, hh, xs, True)

    def final_relay(idx, hh, xs, begin):
        source = lo * 4 + x
        for q in range(4):
            for part, (a, rows, quarter, at) in enumerate(B_PARTS[q]):
                here = jnp.logical_and(
                    jnp.logical_and(hh == yh, xs == x), jnp.logical_and(r == quarter, relay == q)
                )
                gone = jnp.logical_and(relay == q, jnp.logical_not(here))
                src, dst = tout.at[0, hh, xs, pl.ds(a, rows)], fin_b.at[source, pl.ds(at, rows)]
                send_sem = s_fb.at[idx * 2 + part]
                if begin:
                    @pl.when(gone)
                    def _(src=src, dst=dst, send_sem=send_sem, quarter=quarter):
                        copy_to(
                            src, dst, send_sem, r_fb.at[source], (z * 8 + hh * 4 + xs, quarter)
                        ).start()

                    @pl.when(here)
                    def _(src=src, dst=dst):
                        pltpu.make_async_copy(src, dst, r_fb.at[source]).start()
                else:
                    @pl.when(gone)
                    def _(src=src, send_sem=send_sem):
                        wait_bytes(src, send_sem)

    def send_opposite(cl):
        for o, hh in enumerate(order):
            if cl == 0 and o == 0:
                start(
                    pbuf.at[cl, hh, xo, arows], opp_in.at[cl, o, far_opp_side],
                    b_opp[cl][o] + far_opp_side, far_opp_to,
                )
            else:
                start(pbuf.at[cl, hh, xo, low], opp_in.at[cl, o, 1, low], b_opp[cl][o] + 1, left)
                start(pbuf.at[cl, hh, xo, high], opp_in.at[cl, o, 0, high], b_opp[cl][o], right)

    def send_direct(cl, o, hh):
        def merge(side, xs, part):
            wait_recv(opp_in.at[cl, o, side, part], b_opp[cl][o] + side)
            pbuf[cl, hh, xs, part, :] = (
                pbuf[cl, hh, xs, part, :].astype(F32) + opp_in[cl, o, side, part, :].astype(F32)
            ).astype(BF16)

        if cl == 0 and o == 0:
            @pl.when(inner)
            def _():
                merge(0, xr, arows)
                merge(1, xl, arows)
        else:
            merge(0, xr, high)
            merge(1, xl, low)
        start(pbuf.at[cl, hh, xl, arows], dir_in.at[cl, o, 1], b_dir[cl][o][1], left)
        start(pbuf.at[cl, hh, xr, arows], dir_in.at[cl, o, 0], b_dir[cl][o][0], right)

    def sum_composite(o, hh):
        wait_recv(dir_in.at[0, o, 0], b_dir[0][o][0])
        wait_recv(dir_in.at[0, o, 1], b_dir[0][o][1])
        wp = 4 * hh + x
        n_own = near(wp, w).astype(F32)
        n_left = near(wp, 4 * yh + xl).astype(F32)
        n_right = near(wp, 4 * yh + xr).astype(F32)
        v_own = pbuf[0, hh, x, arows, :].astype(F32)
        v_left = dir_in[0, o, 0].astype(F32)
        v_right = dir_in[0, o, 1].astype(F32)
        znear[o] = n_own * v_own + n_left * v_left + n_right * v_right
        zfar[o] = (1.0 - n_own) * v_own + (1.0 - n_left) * v_left + (1.0 - n_right) * v_right

    def chain_two(o):
        @pl.when(far_role)
        def _():
            chain_out[2, o] = zfar[o].astype(BF16)

        @pl.when(near_role)
        def _():
            wait_recv(chain_in.at[2, o], b_chain[2][o])
            chain_out[2, o] = (zfar[o] + chain_in[2, o].astype(F32)).astype(BF16)

        start(chain_out.at[2, o], chain_in.at[1, o], b_chain[1][o], behind)

    def sum_whole(o, hh):
        wait_recv(dir_in.at[1, o, 0], b_dir[1][o][0])
        wait_recv(dir_in.at[1, o, 1], b_dir[1][o][1])
        zone[o] = (
            pbuf[1, hh, x, arows, :].astype(F32) + dir_in[1, o, 0].astype(F32) + dir_in[1, o, 1].astype(F32)
        )

    def chain_one(o):
        wait_recv(chain_in.at[1, o], b_chain[1][o])
        chain_out[1, o] = (zone[o] + chain_in[1, o].astype(F32)).astype(BF16)
        start(chain_out.at[1, o], chain_in.at[0, o], b_chain[0][o], behind)

    def chain_zero(o, hh):
        wait_recv(chain_in.at[0, o], b_chain[0][o])
        chain_out[0, o] = (znear[o] + chain_in[0, o].astype(F32)).astype(BF16)
        start(chain_out.at[0, o], chain_in.at[2, o], b_chain[2][o], mate, role_cond=far_role)
        for a, rows, quarter, at in A_PARTS:
            src, dst = chain_out.at[0, o, pl.ds(a, rows)], fin_a.at[mine, pl.ds(at, rows)]
            cond = None
            if o == 0:
                cond = not_quarter[quarter]

                @pl.when(jnp.logical_and(near_role, r == quarter))
                def _(src=src, dst=dst):
                    pltpu.make_async_copy(src, dst, recv_sems.at[r_fa + mine]).start()
            start(
                src, dst, r_fa + mine, (z * 8 + hh * 4 + x, quarter), cond=cond, role_cond=near_role
            )

    late = by_role(4, 0)
    relay_from = by_role(2, 8)
    back_events = [
        (10, 2, lambda: send_opposite(0)),
        (38, 26, lambda: chain_zero(0, yh)),
        (16, 10, lambda: send_opposite(1)),
        (28, 13, lambda: sum_composite(1, 1 - yh)),
        (30, 17, lambda: sum_whole(0, yh)),
        (15, 7, lambda: send_direct(0, 0, yh)),
        (23, 11, lambda: sum_composite(0, yh)),
        (44, 29, lambda: chain_zero(1, 1 - yh)),
        (28, 15, lambda: chain_two(1)),
        (35, 23, lambda: chain_one(1)),
        (21, 14, lambda: send_direct(1, 0, yh)),
        (23, 12, lambda: chain_two(0)),
        (26, 15, lambda: send_direct(1, 1, 1 - yh)),
        (18, 8, lambda: send_direct(0, 1, 1 - yh)),
        (34, 22, lambda: sum_whole(1, 1 - yh)),
        (32, 17, lambda: chain_one(0)),
    ]

    def backward_step(t, carry):
        for near_at, far_at, what in back_events:
            pl.when(t == by_role(near_at, far_at))(what)

        c = t - late

        @pl.when(jnp.logical_and(c >= 0, c < 16))
        def _():
            backward_panel(c)

        u = t - relay_from

        @pl.when(jnp.logical_and(u >= 0, u < 40))
        def _():
            relay_backward(u)

        return carry

    lax.fori_loop(0, BWD_STEPS, backward_step, 0)

    for quarter in range(4):
        a_rows = sum(p[1] for p in A_PARTS if p[2] == quarter)

        @pl.when(r == quarter)
        def _(a_rows=a_rows):
            if a_rows:
                part = pl.ds(0, a_rows)
                for source in range(4):
                    wait_recv(fin_a.at[source, part], r_fa + source)
                result = base[part, :]
                for source in range(4):
                    result = result + fin_a[source, part, :].astype(F32)
                both[part, HID:] = result.astype(BF16)
            if a_rows < QR:
                part = pl.ds(a_rows, QR - a_rows)
                for source in range(8):
                    wait_bytes(fin_b.at[source, part], r_fb.at[source])
                result = base[part, :]
                for source in range(8):
                    result = result + fin_b[source, part, :].astype(F32)
                both[part, HID:] = result.astype(BF16)

    drain()
    drain_many(s_rz, 32, RB)
    drain_many(s_src, 7, RB)
    drain_many(s_y, 64, RB)
    drain_many(s_p, 64, RB)
    drain_many(s_t, 32, RB)

    def drain_final(idx, carry):
        hh, n = lax.rem(idx, 2), idx // 2
        xs = lax.rem(x + jnp.where(n == 0, 2, jnp.where(n == 1, 3, jnp.where(n == 2, 1, 0))), 4)
        final_relay(idx, hh, xs, False)
        return carry

    lax.fori_loop(0, 8, drain_final, 0)


def on_device(
    features, degrees, cotangent, self_weight, neigh_weight, bias_vector,
    block_values, block_rows, block_cols, block_count,
):
    vmem = pl.BlockSpec(memory_space=pltpu.VMEM)
    smem = pl.BlockSpec(memory_space=pltpu.SMEM)
    anyspace = pl.BlockSpec(memory_space=pl.ANY)
    panel = (PR, HID)
    apanel = (AR, HID)
    piece = (RB, HID)
    dma = pltpu.SemaphoreType.DMA
    both = pl.pallas_call(
        kernel,
        out_shape=jax.ShapeDtypeStruct((QR, 2 * HID), BF16),
        in_specs=[smem, smem, smem, vmem, vmem, anyspace, vmem, vmem, vmem, anyspace],
        out_specs=vmem,
        scratch_shapes=[
            pltpu.VMEM((16, SLOTS, BLK, BLK), BF16),
            pltpu.VMEM((16, PR, PR), BF16),
            pltpu.VMEM((SLOTS + 1, BLK, BLK), BF16),
            pltpu.VMEM((2, 2, 4) + panel, BF16),
            pltpu.VMEM((2, 2) + apanel, BF16),
            pltpu.VMEM(panel, F32),
            pltpu.VMEM((QR, HID), BF16),
            pltpu.VMEM(panel, F32),
            pltpu.VMEM(panel, BF16),
            pltpu.VMEM((4, QR, HID), BF16),
            pltpu.VMEM(panel, BF16),
            pltpu.VMEM((HID, PR), BF16),
            pltpu.VMEM((QR, HID), F32),
            pltpu.VMEM((5, 2, 4) + piece, BF16),
            pltpu.VMEM((2, 2, 4) + panel, BF16),
            pltpu.VMEM((2, 2, 2) + apanel, BF16),
            pltpu.VMEM((2, 2, 2) + apanel, BF16),
            pltpu.VMEM((2,) + apanel, F32),
            pltpu.VMEM((2,) + apanel, F32),
            pltpu.VMEM((2,) + apanel, F32),
            pltpu.VMEM((3, 2) + apanel, BF16),
            pltpu.VMEM((3, 2) + apanel, BF16),
            pltpu.VMEM((4, QR, HID), BF16),
            pltpu.VMEM((2, 2, 2, 2, 4) + piece, BF16),
            pltpu.VMEM((4, 2, 4) + piece, BF16),
            pltpu.VMEM((5, 2, 4) + piece, BF16),
            pltpu.VMEM(piece, F32),
            pltpu.VMEM((8, QR, HID), BF16),
            dma((128,)),
            dma((128,)),
            dma((2,)),
            pltpu.SemaphoreType.REGULAR,
            dma((32,)),
            dma((40,)),
            dma((7,)),
            dma((64,)),
            dma((16,)),
            dma((64,)),
            dma((64,)),
            dma((32,)),
            dma((32,)),
            dma((16,)),
            dma((8,)),
        ],
        compiler_params=pltpu.CompilerParams(
            collective_id=0, has_side_effects=True, vmem_limit_bytes=60 * 1024 * 1024
        ),
        name="sage_layer",
    )(
        jnp.transpose(block_rows, (2, 0, 1)), jnp.transpose(block_cols, (2, 0, 1)), block_count,
        features, degrees.reshape(NB, BLK), cotangent,
        self_weight, neigh_weight, bias_vector, block_values,
    )
    return both[:, 0:HID], both[:, HID:]


def solution(mesh):
    return jax.shard_map(
        on_device,
        mesh=mesh,
        in_specs=(
            P("rows", None),
            P("rows"),
            P("rows", None),
            P(),
            P(),
            P(),
            P("rows", "rep", None, None, None),
            P("rows", "rep", None),
            P("rows", "rep", None),
            P("rows", "rep"),
        ),
        out_specs=(P(("rows", "rep"), None), P(("rows", "rep"), None)),
        check_vma=False,
    )
```

```python
import jax
import jax.numpy as jnp
from jax import lax
from jax.experimental import pallas as pl
from jax.experimental.pallas import tpu as pltpu
from jax.sharding import PartitionSpec as P

MESH = pl.DeviceIdType.MESH
F32 = jnp.float32
BF16 = jnp.bfloat16
NB = 6
BLK = 128
SLOTS = 12
PR = NB * BLK
HID = 256
QR = PR // 4
RB = 80
AR = PR - 4 * RB
HA = AR // 2
FWD_STEPS = 47
BUILD_FROM = 3
BWD_STEPS = 46


def quarter_parts(start, size):
    parts = []
    for quarter in range(4):
        a, b = max(start, quarter * QR), min(start + size, (quarter + 1) * QR)
        if a < b:
            parts.append((a - start, b - a, quarter, a - quarter * QR))
    return parts


A_PARTS = [quarter_parts(0, HA), quarter_parts(HA, HA)]
B_PARTS = [quarter_parts(AR + q * RB, RB) for q in range(4)]


def kernel(
    rows_s, cols_s, cnt_s, feat_hbm, deg, cot_hbm, wself_hbm, wneigh_hbm, bias, w_hbm,
    both,
    feat, wself, wneigh, wv, dense, merged, xbuf, zbuf, acc, cot, dcol,
    mid_src, mid_in, mid_out, sbuf, sflip, base, rbuf,
    pbuf, opp_in, dir_in, znear, zfar, zone, chain_in, chain_out, fin_a,
    rin, tin, tout, tacc, fin_b,
    send_sems, recv_sems, load_sems, go_sem,
    s_rz, r_rz, s_src, s_y, r_y, s_p, r_p, s_t, r_t, s_fb, r_fb,
):
    i = lax.axis_index("rows")
    r = lax.axis_index("rep")
    z, yh, x, w = i // 8, lax.rem(i // 4, 2), lax.rem(i, 4), lax.rem(i, 8)
    lo, core = r // 2, lax.rem(r, 2)
    role = lax.rem(core + lo, 2)
    step = 1 - 2 * lo
    znext, zprev = lax.rem(z + step + 8, 8), lax.rem(z - step + 8, 8)
    xr, xl, xo = lax.rem(x + 1, 4), lax.rem(x + 3, 4), lax.rem(x + 2, 4)
    inner = jnp.logical_or(x == 1, x == 2)
    near_role, far_role = role == 0, role == 1
    relay = 2 * yh + role
    share = pl.ds(pl.multiple_of(AR + RB * relay, 16), RB)
    share_across = pl.ds(pl.multiple_of(AR + RB * (2 * (1 - yh) + role), 16), RB)

    def dev(z_, yh_, x_, lo_, role_):
        return (z_ * 8 + yh_ * 4 + x_, 2 * lo_ + lax.rem(role_ + lo_, 2))

    left, right = dev(z, yh, xl, lo, role), dev(z, yh, xr, lo, role)
    opposite = dev(z, yh, xo, lo, role)
    ahead, behind = dev(znext, yh, x, lo, role), dev(zprev, yh, x, lo, role)
    mate = dev(z, yh, x, lo, 1 - role)
    across = dev(z, 1 - yh, x, 1 - lo, role)

    def near(wp, w_at, lo_at=lo):
        return lax.rem(jnp.where(wp <= w_at, 1, 0) + lo_at, 2)

    load_feat = pltpu.make_async_copy(feat_hbm, feat, load_sems.at[2])
    load_feat.start()
    load_w = pltpu.make_async_copy(w_hbm.at[0], wv, load_sems.at[0])
    load_w.start()
    load_cot = pltpu.make_async_copy(cot_hbm.at[pl.ds(r * QR, QR)], cot, load_sems.at[1])
    load_cot.start()
    load_self = pltpu.make_async_copy(wself_hbm, wself, load_sems.at[3])
    load_self.start()
    load_neigh = pltpu.make_async_copy(wneigh_hbm, wneigh, load_sems.at[4])
    load_neigh.start()

    barrier = pltpu.get_barrier_semaphore()

    def greet(n, carry):
        at = lax.rem(w * 4 + r + n, 32)
        pl.semaphore_signal(
            barrier, inc=1, device_id=(z * 8 + at // 4, lax.rem(at, 4)), device_id_type=MESH
        )
        return carry

    lax.fori_loop(1, 32, greet, 0)
    pl.semaphore_signal(barrier, inc=1, device_id=ahead, device_id_type=MESH)
    pl.semaphore_signal(barrier, inc=1, device_id=behind, device_id_type=MESH)
    pl.semaphore_wait(barrier, 33)
    load_feat.wait()

    sends, recvs, pending = [0], [0], []

    def recv_slot(n=1):
        recvs[0] += n
        return recvs[0] - n

    def copy_to(src, dst, send_sem, recv_sem, device):
        return pltpu.make_async_remote_copy(
            src_ref=src, dst_ref=dst, send_sem=send_sem, recv_sem=recv_sem,
            device_id=device, device_id_type=MESH,
        )

    def joined(cond, role_cond):
        if cond is None or role_cond is None:
            return role_cond if cond is None else cond
        return jnp.logical_and(cond, role_cond)

    def start(src, dst, slot, device, cond=None, role_cond=None, send_slot=None):
        if send_slot is None:
            send_slot = sends[0]
            sends[0] += 1
        copy = copy_to(src, dst, send_sems.at[send_slot], recv_sems.at[slot], device)
        both = joined(cond, role_cond)
        if both is None:
            copy.start()
        else:
            pl.when(both)(lambda: copy.start())
        pending.append((cond, role_cond, src.shape[-2], send_slot))
        return send_slot

    def wait_bytes(ref, sem):
        pltpu.make_async_copy(ref, ref, sem).wait()

    def wait_recv(ref, slot):
        wait_bytes(ref, recv_sems.at[slot])

    def drain():
        for cond, role_cond, rows, slot in pending:
            cond = joined(cond, role_cond)

            def wait(rows=rows, slot=slot):
                wait_bytes(zbuf.at[0, 0, pl.ds(0, rows)], send_sems.at[slot])

            if cond is None:
                wait()
            else:
                pl.when(cond)(wait)
        pending.clear()

    def drain_many(sems, count, rows):
        def wait(n, carry):
            wait_bytes(zbuf.at[0, 0, pl.ds(0, rows)], sems.at[n])
            return carry

        lax.fori_loop(0, count, wait, 0)

    order = (yh, 1 - yh)
    arows = pl.ds(0, AR)
    low, high = pl.ds(0, HA), pl.ds(HA, HA)

    not_quarter = [r != quarter for quarter in range(4)]
    near_side = [
        [near(4 * hh + x, 4 * yh + nx) == 1 for nx in (xr, xl)] for hh in order
    ]
    far_side = [
        [near(4 * hh + x, 4 * yh + nx) == 0 for nx in (xr, xl)] for hh in order
    ]

    halves = (low, high)

    def slots_for(*counts):
        if not counts:
            return recv_slot()
        return [slots_for(*counts[1:]) for _ in range(counts[0])]

    r_z0, r_z1, r_z2 = slots_for(2, 2), slots_for(2, 2), slots_for(2, 2)
    r_dir = slots_for(2, 2, 2, 2)
    r_opp = slots_for(2, 2, 2)
    comp_slots = [[[None, None], [None, None]], [[None, None], [None, None]]]

    def comp_direct(o, s, hh, idx, src, role_cond=None):
        flags = near_side if idx == 0 else far_side
        for side, target in enumerate((right, left)):
            comp_slots[o][s][side] = start(
                src, xbuf.at[0, hh, x, halves[s]], r_dir[0][o][s][side], target,
                cond=flags[o][side], role_cond=role_cond, send_slot=comp_slots[o][s][side],
            )

    own_b = feat.at[share]
    copy_to(own_b, rbuf.at[1, yh, x], s_rz.at[0], r_rz.at[8], behind).start()
    copy_to(feat.at[share_across], rbuf.at[0, yh, x], s_src.at[0], r_rz.at[1], across).start()
    for n, (target, at) in enumerate(((right, 2), (left, 3), (opposite, 4))):
        copy_to(own_b, rbuf.at[0, yh, x], s_src.at[1 + n], r_rz.at[at], target).start()
    for s, half in enumerate(halves):
        start(feat.at[half], xbuf.at[1, yh, x, half], r_z1[0][s], ahead, role_cond=near_role)
    for s, half in enumerate(halves):
        start(feat.at[half], zbuf.at[0, yh, half], r_z0[1][s], across, role_cond=near_role)
    for s, half in enumerate(halves):
        comp_direct(0, s, yh, 0, feat.at[half], near_role)

    @pl.when(near_role)
    def _():
        zbuf[0, yh] = feat[arows, :]

    rbuf[0, yh, x] = feat[share, :]

    dcol_rows = deg[...].astype(F32)
    dcol_t = jnp.concatenate([dcol_rows, dcol_rows[0:2]], axis=0).T
    for b in range(NB):
        dcol[pl.ds(b * BLK, BLK), :] = jnp.broadcast_to(dcol_t[:, b : b + 1], (BLK, HID))

    acc[...] = jnp.zeros_like(acc)
    merged[SLOTS] = jnp.zeros((BLK, BLK), BF16)

    def block_of(cl, wp):
        return jnp.where(cl == 1, 8 + w - wp, lax.rem(w - wp + 16, 16))

    def build(c):
        cl, hh, xs = forward_place(c)
        wp = 4 * hh + xs
        j = block_of(cl, wp)
        count = cnt_s[0, j]
        places = [
            jnp.where(k < count, rows_s[k, 0, j] * NB + cols_s[k, 0, j], -1) for k in range(SLOTS)
        ]
        for k in range(SLOTS):
            before = SLOTS
            for earlier in range(k):
                before = jnp.where(places[earlier] == places[k], earlier, before)
            merged[k] = wv[j, k] if k == 0 else wv[j, k] + merged[before]
        for b in range(NB):
            for a in range(NB):
                last = SLOTS
                for k in range(SLOTS):
                    last = jnp.where(places[k] == b * NB + a, k, last)
                dense[cl * 8 + wp, pl.ds(b * BLK, BLK), pl.ds(a * BLK, BLK)] = merged[last]

    def forward_place(c):
        cl = jnp.where(c < 8, 1, 0)
        m = lax.rem(c, 8)
        hh = jnp.where(lax.rem(m, 2) == 0, yh, 1 - yh)
        n = m // 2
        xs = lax.rem(x + jnp.where(n == 0, 0, jnp.where(n == 1, 3, jnp.where(n == 2, 1, 2))), 4)
        return cl, hh, xs

    def relay_forward(t):
        kappa, idx = t // 8, lax.rem(t, 8)
        other = jnp.logical_or(idx == 1, idx >= 5)
        hh = jnp.where(other, 1 - yh, yh)
        off = jnp.where(
            idx <= 1, 0,
            jnp.where(
                jnp.logical_or(idx == 2, idx == 5), 3,
                jnp.where(jnp.logical_or(idx == 3, idx == 6), 1, 2),
            ),
        )
        xs = lax.rem(x + off, 4)
        piece = rbuf.at[kappa, hh, xs]

        @pl.when(t > 0)
        def _():
            wait_bytes(piece, r_rz.at[t])

        @pl.when(jnp.logical_and(t > 0, t < 32))
        def _():
            copy_to(piece, rbuf.at[kappa + 1, hh, xs], s_rz.at[t], r_rz.at[t + 8], behind).start()

        @pl.when(t == 1)
        def _():
            for n, (target, at) in enumerate(((right, 5), (left, 6), (opposite, 7))):
                copy_to(
                    rbuf.at[0, 1 - yh, x], rbuf.at[0, 1 - yh, x], s_src.at[4 + n], r_rz.at[at], target
                ).start()

        cl = lax.rem(kappa, 2)
        for n in range(2):
            near_n = near(4 * hh + xs, 4 * n + x, 1 - lo)
            role_n = jnp.where(kappa == 2, near_n, kappa // 3)
            skip = jnp.logical_or(
                jnp.logical_and(kappa == 0, near_n == 0), jnp.logical_and(kappa == 4, near_n == 1)
            )

            @pl.when(jnp.logical_not(skip))
            def _(n=n, role_n=role_n):
                copy_to(
                    piece, xbuf.at[cl, hh, xs, share], s_y.at[n * 32 + lax.rem(t, 32)],
                    r_y.at[cl * 8 + hh * 4 + xs], dev(z, n, x, 1 - lo, role_n),
                ).start()

    def forward_panel(c):
        cl, hh, xs = forward_place(c)
        at = cl * 8 + hh * 4 + xs
        wait_bytes(xbuf.at[cl, hh, xs, pl.ds(AR, 4 * RB)], r_y.at[at])
        acc[...] += jnp.dot(dense[at], xbuf[cl, hh, xs], preferred_element_type=F32)

    def got_z0(o, s, hh):
        piece = zbuf.at[0, hh, halves[s]]
        role_cond = far_role if o == 0 else None
        wait_recv(piece, r_z0[o][s])
        start(piece, xbuf.at[1, hh, x, halves[s]], r_z1[o][s], ahead, role_cond=role_cond)
        comp_direct(o, s, hh, 0, piece, role_cond)

    def got_z1(o, s, hh):
        piece = xbuf.at[1, hh, x, halves[s]]
        wait_recv(piece, r_z1[o][s])
        start(piece, zbuf.at[1, hh, halves[s]], r_z2[o][s], ahead)
        start(piece, piece, r_dir[1][o][s][0], right)
        start(piece, piece, r_dir[1][o][s][1], left)

    def got_z2(o, s, hh):
        piece = zbuf.at[1, hh, halves[s]]
        wait_recv(piece, r_z2[o][s])
        start(piece, zbuf.at[0, hh, halves[s]], r_z0[o][s], mate, role_cond=near_role)
        comp_direct(o, s, hh, 1, piece)
        own = near(4 * hh + x, w)
        xbuf[0, hh, x, halves[s], :] = zbuf[1 - own, hh, halves[s], :]

    def pass_opposite(cl, o, s, hh):
        whole = cl == 0 and o == 0
        cond = inner if whole else None
        for side, (xs, target) in enumerate(((xl, right), (xr, left))):
            piece = xbuf.at[cl, hh, xs, halves[s]]
            wait_recv(piece, r_dir[cl][o][s][side])
            if whole or s == side:
                start(piece, piece, r_opp[cl][o][s], target, cond=cond)

    def wait_opposite(cl, o, s, hh):
        wait_recv(xbuf.at[cl, hh, xo, halves[s]], r_opp[cl][o][s])

    def by_role(near_at, far_at):
        return jnp.where(near_role, near_at, far_at)

    events = [
        (-1, 12, lambda: got_z0(0, 0, order[0])),
        (38, 43, lambda: wait_opposite(0, 1, 1, order[1])),
        (4, 15, lambda: got_z0(1, 0, order[1])),
        (4, 17, lambda: got_z0(1, 1, order[1])),
        (4, 18, lambda: got_z1(0, 0, order[0])),
        (25, 36, lambda: pass_opposite(0, 1, 1, order[1])),
        (7, 23, lambda: got_z1(1, 0, order[1])),
        (14, 27, lambda: got_z2(1, 0, order[1])),
        (11, 24, lambda: got_z2(0, 0, order[0])),
        (11, 24, lambda: got_z2(0, 1, order[0])),
        (9, 23, lambda: got_z1(1, 1, order[1])),
        (16, 30, lambda: got_z2(1, 1, order[1])),
        (12, 28, lambda: pass_opposite(1, 0, 0, order[0])),
        (13, 30, lambda: pass_opposite(1, 0, 1, order[0])),
        (4, 21, lambda: got_z1(0, 1, order[0])),
        (17, 32, lambda: pass_opposite(1, 1, 1, order[1])),
        (29, 37, lambda: wait_opposite(1, 1, 0, order[1])),
        (16, 30, lambda: pass_opposite(1, 1, 0, order[1])),
        (24, 39, lambda: pass_opposite(0, 1, 0, order[1])),
        (19, 35, lambda: pass_opposite(0, 0, 1, order[0])),
        (23, 36, lambda: wait_opposite(1, 0, 1, order[0])),
        (24, 35, lambda: wait_opposite(1, 0, 0, order[0])),
        (28, 33, lambda: pass_opposite(0, 0, 0, order[0])),
        (26, 37, lambda: wait_opposite(1, 1, 1, order[1])),
        (35, 39, lambda: wait_opposite(0, 0, 0, order[0])),
        (-1, 14, lambda: got_z0(0, 1, order[0])),
        (32, 45, lambda: wait_opposite(0, 1, 0, order[1])),
        (30, 40, lambda: wait_opposite(0, 0, 1, order[0])),
    ]
    compute_from = by_role(24, 31)

    def forward_step(t, carry):
        for near_at, far_at, what in events:
            pl.when(t == by_role(near_at, far_at))(what)

        @pl.when(t < 40)
        def _():
            relay_forward(t)

        @pl.when(t == BUILD_FROM)
        def _():
            load_w.wait()

        @pl.when(jnp.logical_and(t >= BUILD_FROM, t < BUILD_FROM + 16))
        def _():
            build(t - BUILD_FROM)

        c = t - compute_from

        @pl.when(jnp.logical_and(c >= 0, c < 16))
        def _():
            forward_panel(c)

        return carry

    lax.fori_loop(0, FWD_STEPS, forward_step, 0)

    mid_src[...] = acc[...].astype(BF16)
    r_mid, r_sc = recv_slot(3), recv_slot(3)
    core_mate, chip_mate = (i, 2 * lo + 1 - core), (i, 2 * (1 - lo) + core)

    def quarter_rows(lo_, core_):
        return pl.ds(pl.multiple_of((2 * lo_ + core_) * QR, QR), QR)

    for lo_ in (1 - lo, lo):
        start(mid_src.at[quarter_rows(lo_, 1 - core)], mid_in.at[lo_], r_mid + lo_, core_mate)
    wait_recv(mid_in.at[1 - lo], r_mid + 1 - lo)
    mid_out[...] = (
        acc[quarter_rows(1 - lo, core), :] + mid_in[1 - lo].astype(F32)
    ).astype(BF16)
    start(mid_out, mid_in.at[2], r_mid + 2, chip_mate)
    own_rows = pl.ds(pl.multiple_of(r * QR, QR), QR)
    load_self.wait()
    load_neigh.wait()
    total = acc[own_rows, :]
    f_own = feat[own_rows, :]
    divisor = dcol[own_rows, :]
    preact = jnp.dot(f_own, wself[...], preferred_element_type=F32) + bias[...].astype(F32)[None, :]
    load_cot.wait()
    wait_recv(mid_in.at[lo], r_mid + lo)
    total = total + mid_in[lo].astype(F32)
    wait_recv(mid_in.at[2], r_mid + 2)
    total = total + mid_in[2].astype(F32)
    neighbours = (total / divisor).astype(BF16)
    preact = preact + jnp.dot(neighbours, wneigh[...], preferred_element_type=F32)
    sig = jax.nn.sigmoid(preact)
    slope = sig * (1.0 + preact * (1.0 - sig))
    pre_grad = (cot[...].astype(F32) * slope).astype(BF16)
    contract = (((1,), (1,)), ((), ()))
    scaled = lax.dot_general(pre_grad, wneigh[...], contract, preferred_element_type=F32)
    sbuf[own_rows, :] = (scaled / divisor).astype(BF16)
    start(sbuf.at[own_rows], sbuf.at[own_rows], r_sc, chip_mate)
    start(sbuf.at[own_rows], sbuf.at[own_rows], r_sc + 1, core_mate)
    both[:, 0:HID] = (preact * sig).astype(BF16)
    base[...] = lax.dot_general(pre_grad, wself[...], contract, preferred_element_type=F32)
    passed_on = sbuf.at[quarter_rows(1 - lo, core)]
    wait_recv(passed_on, r_sc)
    start(passed_on, passed_on, r_sc + 2, core_mate)
    wait_recv(sbuf.at[quarter_rows(lo, 1 - core)], r_sc + 1)
    wait_recv(sbuf.at[quarter_rows(1 - lo, 1 - core)], r_sc + 2)
    sflip[...] = sbuf[...].T

    b_opp = [[recv_slot(2) for o in range(2)] for cl in range(2)]
    b_dir = [[[recv_slot() for _ in range(2)] for _ in order] for _ in range(2)]
    b_chain = slots_for(3, 2, 2)
    r_fa = recv_slot(4)
    mine = 2 * lo + yh
    far_opp_side = jnp.where(x <= 1, 0, 1)
    far_opp_to = dev(z, yh, jnp.where(x <= 1, xr, xl), lo, role)

    def backward_panel(c):
        cl = jnp.where(c < 8, 0, 1)
        m = lax.rem(c, 8)
        hh, n = lax.rem(m, 2), m // 2
        xs = lax.rem(x + jnp.where(n == 0, 2, jnp.where(n == 1, 3, jnp.where(n == 2, 1, 0))), 4)
        at = cl * 8 + hh * 4 + xs
        flipped = jnp.dot(sflip[...], dense[at], preferred_element_type=F32)
        pbuf[cl, hh, xs] = flipped.astype(BF16).T
        for q in range(4):
            copy_to(
                pbuf.at[cl, hh, xs, pl.ds(AR + RB * q, RB)], rin.at[yh, role, cl, hh, xs],
                s_p.at[at * 4 + q], r_p.at[(yh * 2 + role) * 16 + at],
                dev(z, q // 2, x, 1 - lo, q % 2),
            ).start()

    def relay_backward(u):
        kappa, idx = 4 - u // 8, lax.rem(u, 8)
        hh, n = lax.rem(idx, 2), idx // 2
        xs = lax.rem(x + jnp.where(n == 0, 2, jnp.where(n == 1, 3, jnp.where(n == 2, 1, 0))), 4)
        cl = lax.rem(kappa, 2)
        tacc[...] = jnp.zeros_like(tacc)
        for n in range(2):
            near_n = near(4 * hh + xs, 4 * n + x, 1 - lo)
            role_n = jnp.where(kappa == 2, near_n, kappa // 3)
            skip = jnp.logical_or(
                jnp.logical_and(kappa == 0, near_n == 0), jnp.logical_and(kappa == 4, near_n == 1)
            )

            @pl.when(jnp.logical_not(skip))
            def _(n=n, role_n=role_n):
                wait_bytes(
                    rin.at[n, role_n, cl, hh, xs], r_p.at[(n * 2 + role_n) * 16 + cl * 8 + hh * 4 + xs]
                )
                tacc[...] += rin[n, role_n, cl, hh, xs].astype(F32)

        @pl.when(u >= 8)
        def _():
            wait_bytes(tin.at[kappa, hh, xs], r_t.at[u - 8])
            tacc[...] += tin[kappa, hh, xs].astype(F32)

        tout[kappa, hh, xs] = tacc[...].astype(BF16)

        @pl.when(u < 32)
        def _():
            copy_to(tout.at[kappa, hh, xs], tin.at[kappa - 1, hh, xs], s_t.at[u], r_t.at[u], ahead).start()

        @pl.when(u >= 32)
        def _():
            final_relay(idx, hh, xs, True)

    def final_relay(idx, hh, xs, begin):
        source = lo * 4 + x
        for q in range(4):
            for part, (a, rows, quarter, at) in enumerate(B_PARTS[q]):
                here = jnp.logical_and(
                    jnp.logical_and(hh == yh, xs == x), jnp.logical_and(r == quarter, relay == q)
                )
                gone = jnp.logical_and(relay == q, jnp.logical_not(here))
                src, dst = tout.at[0, hh, xs, pl.ds(a, rows)], fin_b.at[source, pl.ds(at, rows)]
                send_sem = s_fb.at[idx * 2 + part]
                if begin:
                    @pl.when(gone)
                    def _(src=src, dst=dst, send_sem=send_sem, quarter=quarter):
                        copy_to(
                            src, dst, send_sem, r_fb.at[source], (z * 8 + hh * 4 + xs, quarter)
                        ).start()

                    @pl.when(here)
                    def _(src=src, dst=dst):
                        pltpu.make_async_copy(src, dst, r_fb.at[source]).start()
                else:
                    @pl.when(gone)
                    def _(src=src, send_sem=send_sem):
                        wait_bytes(src, send_sem)

    def send_opposite(cl):
        for o, hh in enumerate(order):
            if cl == 0 and o == 0:
                start(
                    pbuf.at[cl, hh, xo, arows], opp_in.at[cl, o, far_opp_side],
                    b_opp[cl][o] + far_opp_side, far_opp_to,
                )
            else:
                start(pbuf.at[cl, hh, xo, low], opp_in.at[cl, o, 1, low], b_opp[cl][o] + 1, left)
                start(pbuf.at[cl, hh, xo, high], opp_in.at[cl, o, 0, high], b_opp[cl][o], right)

    def send_direct(cl, o, hh):
        def merge(side, xs, part):
            wait_recv(opp_in.at[cl, o, side, part], b_opp[cl][o] + side)
            pbuf[cl, hh, xs, part, :] = (
                pbuf[cl, hh, xs, part, :].astype(F32) + opp_in[cl, o, side, part, :].astype(F32)
            ).astype(BF16)

        if cl == 0 and o == 0:
            @pl.when(inner)
            def _():
                merge(0, xr, arows)
                merge(1, xl, arows)
        else:
            merge(0, xr, high)
            merge(1, xl, low)
        start(pbuf.at[cl, hh, xl, arows], dir_in.at[cl, o, 1], b_dir[cl][o][1], left)
        start(pbuf.at[cl, hh, xr, arows], dir_in.at[cl, o, 0], b_dir[cl][o][0], right)

    def sum_composite(o, hh):
        wait_recv(dir_in.at[0, o, 0], b_dir[0][o][0])
        wait_recv(dir_in.at[0, o, 1], b_dir[0][o][1])
        wp = 4 * hh + x
        n_own = near(wp, w).astype(F32)
        n_left = near(wp, 4 * yh + xl).astype(F32)
        n_right = near(wp, 4 * yh + xr).astype(F32)
        v_own = pbuf[0, hh, x, arows, :].astype(F32)
        v_left = dir_in[0, o, 0].astype(F32)
        v_right = dir_in[0, o, 1].astype(F32)
        znear[o] = n_own * v_own + n_left * v_left + n_right * v_right
        zfar[o] = (1.0 - n_own) * v_own + (1.0 - n_left) * v_left + (1.0 - n_right) * v_right

    def chain_two(o, s):
        half = halves[s]

        @pl.when(far_role)
        def _():
            chain_out[2, o, half, :] = zfar[o, half, :].astype(BF16)

        @pl.when(near_role)
        def _():
            wait_recv(chain_in.at[2, o, half], b_chain[2][o][s])
            chain_out[2, o, half, :] = (
                zfar[o, half, :] + chain_in[2, o, half, :].astype(F32)
            ).astype(BF16)

        start(chain_out.at[2, o, half], chain_in.at[1, o, half], b_chain[1][o][s], behind)

    def sum_whole(o, hh):
        wait_recv(dir_in.at[1, o, 0], b_dir[1][o][0])
        wait_recv(dir_in.at[1, o, 1], b_dir[1][o][1])
        zone[o] = (
            pbuf[1, hh, x, arows, :].astype(F32) + dir_in[1, o, 0].astype(F32) + dir_in[1, o, 1].astype(F32)
        )

    def chain_one(o, s):
        half = halves[s]
        wait_recv(chain_in.at[1, o, half], b_chain[1][o][s])
        chain_out[1, o, half, :] = (
            zone[o, half, :] + chain_in[1, o, half, :].astype(F32)
        ).astype(BF16)
        start(chain_out.at[1, o, half], chain_in.at[0, o, half], b_chain[0][o][s], behind)

    def chain_zero(o, s, hh):
        half = halves[s]
        wait_recv(chain_in.at[0, o, half], b_chain[0][o][s])
        chain_out[0, o, half, :] = (
            znear[o, half, :] + chain_in[0, o, half, :].astype(F32)
        ).astype(BF16)
        start(
            chain_out.at[0, o, half], chain_in.at[2, o, half], b_chain[2][o][s], mate, role_cond=far_role
        )
        for a, rows, quarter, at in A_PARTS[s]:
            src = chain_out.at[0, o, pl.ds(s * HA + a, rows)]
            dst = fin_a.at[mine, pl.ds(at, rows)]
            cond = None
            if o == 0:
                cond = not_quarter[quarter]

                @pl.when(jnp.logical_and(near_role, r == quarter))
                def _(src=src, dst=dst):
                    pltpu.make_async_copy(src, dst, recv_sems.at[r_fa + mine]).start()
            start(
                src, dst, r_fa + mine, (z * 8 + hh * 4 + x, quarter), cond=cond, role_cond=near_role
            )

    late = by_role(5, 0)
    relay_from = by_role(2, 6)
    back_events = [
        (10, 2, lambda: send_opposite(0)),
        (30, 17, lambda: sum_whole(0, yh)),
        (38, 26, lambda: chain_zero(0, 1, yh)),
        (16, 10, lambda: send_opposite(1)),
        (28, 14, lambda: sum_composite(1, 1 - yh)),
        (37, 24, lambda: chain_zero(0, 0, yh)),
        (17, 7, lambda: send_direct(0, 0, yh)),
        (23, 11, lambda: sum_composite(0, yh)),
        (38, 28, lambda: chain_zero(1, 0, 1 - yh)),
        (38, 29, lambda: chain_zero(1, 1, 1 - yh)),
        (28, 16, lambda: chain_two(1, 0)),
        (28, 15, lambda: chain_two(1, 1)),
        (35, 23, lambda: chain_one(1, 0)),
        (35, 24, lambda: chain_one(1, 1)),
        (19, 8, lambda: send_direct(0, 1, 1 - yh)),
        (23, 14, lambda: chain_two(0, 0)),
        (26, 11, lambda: chain_two(0, 1)),
        (25, 15, lambda: send_direct(1, 1, 1 - yh)),
        (20, 14, lambda: send_direct(1, 0, yh)),
        (33, 18, lambda: chain_one(0, 1)),
        (30, 17, lambda: chain_one(0, 0)),
        (34, 22, lambda: sum_whole(1, 1 - yh)),
    ]

    def backward_step(t, carry):
        for near_at, far_at, what in back_events:
            pl.when(t == by_role(near_at, far_at))(what)

        c = t - late

        @pl.when(jnp.logical_and(c >= 0, c < 16))
        def _():
            backward_panel(c)

        u = t - relay_from

        @pl.when(jnp.logical_and(u >= 0, u < 40))
        def _():
            relay_backward(u)

        return carry

    lax.fori_loop(0, BWD_STEPS, backward_step, 0)

    for quarter in range(4):
        a_rows = sum(p[1] for parts in A_PARTS for p in parts if p[2] == quarter)

        @pl.when(r == quarter)
        def _(a_rows=a_rows):
            if a_rows:
                part = pl.ds(0, a_rows)
                for source in range(4):
                    wait_recv(fin_a.at[source, part], r_fa + source)
                result = base[part, :]
                for source in range(4):
                    result = result + fin_a[source, part, :].astype(F32)
                both[part, HID:] = result.astype(BF16)
            if a_rows < QR:
                part = pl.ds(a_rows, QR - a_rows)
                for source in range(8):
                    wait_bytes(fin_b.at[source, part], r_fb.at[source])
                result = base[part, :]
                for source in range(8):
                    result = result + fin_b[source, part, :].astype(F32)
                both[part, HID:] = result.astype(BF16)

    drain()
    drain_many(s_rz, 32, RB)
    drain_many(s_src, 7, RB)
    drain_many(s_y, 64, RB)
    drain_many(s_p, 64, RB)
    drain_many(s_t, 32, RB)

    def drain_final(idx, carry):
        hh, n = lax.rem(idx, 2), idx // 2
        xs = lax.rem(x + jnp.where(n == 0, 2, jnp.where(n == 1, 3, jnp.where(n == 2, 1, 0))), 4)
        final_relay(idx, hh, xs, False)
        return carry

    lax.fori_loop(0, 8, drain_final, 0)


def on_device(
    features, degrees, cotangent, self_weight, neigh_weight, bias_vector,
    block_values, block_rows, block_cols, block_count,
):
    vmem = pl.BlockSpec(memory_space=pltpu.VMEM)
    smem = pl.BlockSpec(memory_space=pltpu.SMEM)
    anyspace = pl.BlockSpec(memory_space=pl.ANY)
    panel = (PR, HID)
    apanel = (AR, HID)
    piece = (RB, HID)
    dma = pltpu.SemaphoreType.DMA
    both = pl.pallas_call(
        kernel,
        out_shape=jax.ShapeDtypeStruct((QR, 2 * HID), BF16),
        in_specs=[smem, smem, smem, anyspace, vmem, anyspace, anyspace, anyspace, vmem, anyspace],
        out_specs=vmem,
        scratch_shapes=[
            pltpu.VMEM(panel, BF16),
            pltpu.VMEM((HID, HID), BF16),
            pltpu.VMEM((HID, HID), BF16),
            pltpu.VMEM((16, SLOTS, BLK, BLK), BF16),
            pltpu.VMEM((16, PR, PR), BF16),
            pltpu.VMEM((SLOTS + 1, BLK, BLK), BF16),
            pltpu.VMEM((2, 2, 4) + panel, BF16),
            pltpu.VMEM((2, 2) + apanel, BF16),
            pltpu.VMEM(panel, F32),
            pltpu.VMEM((QR, HID), BF16),
            pltpu.VMEM(panel, F32),
            pltpu.VMEM(panel, BF16),
            pltpu.VMEM((3, QR, HID), BF16),
            pltpu.VMEM((QR, HID), BF16),
            pltpu.VMEM(panel, BF16),
            pltpu.VMEM((HID, PR), BF16),
            pltpu.VMEM((QR, HID), F32),
            pltpu.VMEM((5, 2, 4) + piece, BF16),
            pltpu.VMEM((2, 2, 4) + panel, BF16),
            pltpu.VMEM((2, 2, 2) + apanel, BF16),
            pltpu.VMEM((2, 2, 2) + apanel, BF16),
            pltpu.VMEM((2,) + apanel, F32),
            pltpu.VMEM((2,) + apanel, F32),
            pltpu.VMEM((2,) + apanel, F32),
            pltpu.VMEM((3, 2) + apanel, BF16),
            pltpu.VMEM((3, 2) + apanel, BF16),
            pltpu.VMEM((4, QR, HID), BF16),
            pltpu.VMEM((2, 2, 2, 2, 4) + piece, BF16),
            pltpu.VMEM((4, 2, 4) + piece, BF16),
            pltpu.VMEM((5, 2, 4) + piece, BF16),
            pltpu.VMEM(piece, F32),
            pltpu.VMEM((8, QR, HID), BF16),
            dma((128,)),
            dma((128,)),
            dma((5,)),
            pltpu.SemaphoreType.REGULAR,
            dma((32,)),
            dma((40,)),
            dma((7,)),
            dma((64,)),
            dma((16,)),
            dma((64,)),
            dma((64,)),
            dma((32,)),
            dma((32,)),
            dma((16,)),
            dma((8,)),
        ],
        compiler_params=pltpu.CompilerParams(
            collective_id=0, has_side_effects=True, vmem_limit_bytes=60 * 1024 * 1024
        ),
        name="sage_layer",
    )(
        jnp.transpose(block_rows, (2, 0, 1)), jnp.transpose(block_cols, (2, 0, 1)), block_count,
        features, degrees.reshape(NB, BLK), cotangent,
        self_weight, neigh_weight, bias_vector, block_values,
    )
    return both[:, 0:HID], both[:, HID:]


def solution(mesh):
    return jax.shard_map(
        on_device,
        mesh=mesh,
        in_specs=(
            P("rows", None),
            P("rows"),
            P("rows", None),
            P(),
            P(),
            P(),
            P("rows", "rep", None, None, None),
            P("rows", "rep", None),
            P("rows", "rep", None),
            P("rows", "rep"),
        ),
        out_specs=(P(("rows", "rep"), None), P(("rows", "rep"), None)),
        check_vma=False,
    )
```

```python
import jax
import jax.numpy as jnp
from jax import lax
from jax.experimental import pallas as pl
from jax.experimental.pallas import tpu as pltpu
from jax.sharding import PartitionSpec as P

MESH = pl.DeviceIdType.MESH
F32 = jnp.float32
BF16 = jnp.bfloat16
NB = 6
BLK = 128
SLOTS = 12
PR = NB * BLK
HID = 256
QR = PR // 4
RB = 80
AR = PR - 4 * RB
HA = AR // 2
FWD_STEPS = 47
BUILD_FROM = 3
BWD_STEPS = 46


def quarter_parts(start, size):
    parts = []
    for quarter in range(4):
        a, b = max(start, quarter * QR), min(start + size, (quarter + 1) * QR)
        if a < b:
            parts.append((a - start, b - a, quarter, a - quarter * QR))
    return parts


A_PARTS = [quarter_parts(0, HA), quarter_parts(HA, HA)]
B_PARTS = [quarter_parts(AR + q * RB, RB) for q in range(4)]


def kernel(
    rows_s, cols_s, cnt_s, feat_hbm, deg, cot_hbm, wself_hbm, wneigh_hbm, bias, w_hbm,
    both,
    feat, wself, wneigh, wv, dense, merged, xbuf, zbuf, acc, cot, dcol,
    mid_src, mid_in, mid_out, sbuf, sflip, base, rbuf,
    pbuf, opp_in, dir_in, znear, zfar, zone, chain_in, chain_out, fin_a,
    rin, tin, tout, tacc, fin_b,
    send_sems, recv_sems, load_sems, go_sem,
    s_rz, r_rz, s_src, s_y, r_y, s_p, r_p, s_t, r_t, s_fb, r_fb,
):
    i = lax.axis_index("rows")
    r = lax.axis_index("rep")
    z, yh, x, w = i // 8, lax.rem(i // 4, 2), lax.rem(i, 4), lax.rem(i, 8)
    lo, core = r // 2, lax.rem(r, 2)
    role = lax.rem(core + lo, 2)
    step = 1 - 2 * lo
    znext, zprev = lax.rem(z + step + 8, 8), lax.rem(z - step + 8, 8)
    xr, xl, xo = lax.rem(x + 1, 4), lax.rem(x + 3, 4), lax.rem(x + 2, 4)
    inner = jnp.logical_or(x == 1, x == 2)
    near_role, far_role = role == 0, role == 1
    relay = 2 * yh + role
    share = pl.ds(pl.multiple_of(AR + RB * relay, 16), RB)
    share_across = pl.ds(pl.multiple_of(AR + RB * (2 * (1 - yh) + role), 16), RB)

    def dev(z_, yh_, x_, lo_, role_):
        return (z_ * 8 + yh_ * 4 + x_, 2 * lo_ + lax.rem(role_ + lo_, 2))

    left, right = dev(z, yh, xl, lo, role), dev(z, yh, xr, lo, role)
    opposite = dev(z, yh, xo, lo, role)
    ahead, behind = dev(znext, yh, x, lo, role), dev(zprev, yh, x, lo, role)
    mate = dev(z, yh, x, lo, 1 - role)
    across = dev(z, 1 - yh, x, 1 - lo, role)

    def near(wp, w_at, lo_at=lo):
        return lax.rem(jnp.where(wp <= w_at, 1, 0) + lo_at, 2)

    load_feat = pltpu.make_async_copy(feat_hbm, feat, load_sems.at[2])
    load_feat.start()
    load_w = pltpu.make_async_copy(w_hbm.at[0], wv, load_sems.at[0])
    load_w.start()
    load_cot = pltpu.make_async_copy(cot_hbm.at[pl.ds(r * QR, QR)], cot, load_sems.at[1])
    load_cot.start()
    load_self = pltpu.make_async_copy(wself_hbm, wself, load_sems.at[3])
    load_self.start()
    load_neigh = pltpu.make_async_copy(wneigh_hbm, wneigh, load_sems.at[4])
    load_neigh.start()

    barrier = pltpu.get_barrier_semaphore()

    def greet(n, carry):
        at = lax.rem(w * 4 + r + n, 32)
        pl.semaphore_signal(
            barrier, inc=1, device_id=(z * 8 + at // 4, lax.rem(at, 4)), device_id_type=MESH
        )
        return carry

    lax.fori_loop(1, 32, greet, 0)
    pl.semaphore_signal(barrier, inc=1, device_id=ahead, device_id_type=MESH)
    pl.semaphore_signal(barrier, inc=1, device_id=behind, device_id_type=MESH)
    pl.semaphore_wait(barrier, 33)
    load_feat.wait()

    sends, recvs, pending = [0], [0], []

    def recv_slot(n=1):
        recvs[0] += n
        return recvs[0] - n

    def copy_to(src, dst, send_sem, recv_sem, device):
        return pltpu.make_async_remote_copy(
            src_ref=src, dst_ref=dst, send_sem=send_sem, recv_sem=recv_sem,
            device_id=device, device_id_type=MESH,
        )

    def joined(cond, role_cond):
        if cond is None or role_cond is None:
            return role_cond if cond is None else cond
        return jnp.logical_and(cond, role_cond)

    def start(src, dst, slot, device, cond=None, role_cond=None, send_slot=None):
        if send_slot is None:
            send_slot = sends[0]
            sends[0] += 1
        copy = copy_to(src, dst, send_sems.at[send_slot], recv_sems.at[slot], device)
        both = joined(cond, role_cond)
        if both is None:
            copy.start()
        else:
            pl.when(both)(lambda: copy.start())
        pending.append((cond, role_cond, src.shape[-2], send_slot))
        return send_slot

    def wait_bytes(ref, sem):
        pltpu.make_async_copy(ref, ref, sem).wait()

    def wait_recv(ref, slot):
        wait_bytes(ref, recv_sems.at[slot])

    def drain():
        for cond, role_cond, rows, slot in pending:
            cond = joined(cond, role_cond)

            def wait(rows=rows, slot=slot):
                wait_bytes(zbuf.at[0, 0, pl.ds(0, rows)], send_sems.at[slot])

            if cond is None:
                wait()
            else:
                pl.when(cond)(wait)
        pending.clear()

    def drain_many(sems, count, rows):
        def wait(n, carry):
            wait_bytes(zbuf.at[0, 0, pl.ds(0, rows)], sems.at[n])
            return carry

        lax.fori_loop(0, count, wait, 0)

    order = (yh, 1 - yh)
    arows = pl.ds(0, AR)
    low, high = pl.ds(0, HA), pl.ds(HA, HA)

    not_quarter = [r != quarter for quarter in range(4)]
    near_side = [
        [near(4 * hh + x, 4 * yh + nx) == 1 for nx in (xr, xl)] for hh in order
    ]
    far_side = [
        [near(4 * hh + x, 4 * yh + nx) == 0 for nx in (xr, xl)] for hh in order
    ]

    halves = (low, high)

    def slots_for(*counts):
        if not counts:
            return recv_slot()
        return [slots_for(*counts[1:]) for _ in range(counts[0])]

    r_z0, r_z1, r_z2 = slots_for(2, 2), slots_for(2, 2), slots_for(2, 2)
    r_dir = slots_for(2, 2, 2, 2)
    r_opp = slots_for(2, 2, 2)
    comp_slots = [[[None, None], [None, None]], [[None, None], [None, None]]]

    def comp_direct(o, s, hh, idx, src, role_cond=None):
        flags = near_side if idx == 0 else far_side
        for side, target in enumerate((right, left)):
            comp_slots[o][s][side] = start(
                src, xbuf.at[0, hh, x, halves[s]], r_dir[0][o][s][side], target,
                cond=flags[o][side], role_cond=role_cond, send_slot=comp_slots[o][s][side],
            )

    own_b = feat.at[share]
    copy_to(own_b, rbuf.at[1, yh, x], s_rz.at[0], r_rz.at[8], behind).start()
    copy_to(feat.at[share_across], rbuf.at[0, yh, x], s_src.at[0], r_rz.at[1], across).start()
    for n, (target, at) in enumerate(((right, 2), (left, 3), (opposite, 4))):
        copy_to(own_b, rbuf.at[0, yh, x], s_src.at[1 + n], r_rz.at[at], target).start()
    for s, half in enumerate(halves):
        start(feat.at[half], xbuf.at[1, yh, x, half], r_z1[0][s], ahead, role_cond=near_role)
    for s, half in enumerate(halves):
        start(feat.at[half], zbuf.at[0, yh, half], r_z0[1][s], across, role_cond=near_role)
    for s, half in enumerate(halves):
        comp_direct(0, s, yh, 0, feat.at[half], near_role)

    @pl.when(near_role)
    def _():
        zbuf[0, yh] = feat[arows, :]

    rbuf[0, yh, x] = feat[share, :]

    dcol_rows = deg[...].astype(F32)
    dcol_t = jnp.concatenate([dcol_rows, dcol_rows[0:2]], axis=0).T
    for b in range(NB):
        dcol[pl.ds(b * BLK, BLK), :] = jnp.broadcast_to(dcol_t[:, b : b + 1], (BLK, BLK))

    acc[...] = jnp.zeros_like(acc)
    merged[SLOTS] = jnp.zeros((BLK, BLK), BF16)

    def block_of(cl, wp):
        return jnp.where(cl == 1, 8 + w - wp, lax.rem(w - wp + 16, 16))

    def build(c):
        cl, hh, xs = forward_place(c)
        wp = 4 * hh + xs
        j = block_of(cl, wp)
        count = cnt_s[0, j]
        places = [
            jnp.where(k < count, rows_s[k, 0, j] * NB + cols_s[k, 0, j], -1) for k in range(SLOTS)
        ]
        for k in range(SLOTS):
            before = SLOTS
            for earlier in range(k):
                before = jnp.where(places[earlier] == places[k], earlier, before)
            merged[k] = wv[j, k] if k == 0 else wv[j, k] + merged[before]
        for b in range(NB):
            for a in range(NB):
                last = SLOTS
                for k in range(SLOTS):
                    last = jnp.where(places[k] == b * NB + a, k, last)
                dense[cl * 8 + wp, pl.ds(b * BLK, BLK), pl.ds(a * BLK, BLK)] = merged[last]

    def forward_place(c):
        cl = jnp.where(c < 8, 1, 0)
        m = lax.rem(c, 8)
        hh = jnp.where(lax.rem(m, 2) == 0, yh, 1 - yh)
        n = m // 2
        xs = lax.rem(x + jnp.where(n == 0, 0, jnp.where(n == 1, 3, jnp.where(n == 2, 1, 2))), 4)
        return cl, hh, xs

    def relay_forward(t):
        kappa, idx = t // 8, lax.rem(t, 8)
        other = jnp.logical_or(idx == 1, idx >= 5)
        hh = jnp.where(other, 1 - yh, yh)
        off = jnp.where(
            idx <= 1, 0,
            jnp.where(
                jnp.logical_or(idx == 2, idx == 5), 3,
                jnp.where(jnp.logical_or(idx == 3, idx == 6), 1, 2),
            ),
        )
        xs = lax.rem(x + off, 4)
        piece = rbuf.at[kappa, hh, xs]

        @pl.when(t > 0)
        def _():
            wait_bytes(piece, r_rz.at[t])

        @pl.when(jnp.logical_and(t > 0, t < 32))
        def _():
            copy_to(piece, rbuf.at[kappa + 1, hh, xs], s_rz.at[t], r_rz.at[t + 8], behind).start()

        @pl.when(t == 1)
        def _():
            for n, (target, at) in enumerate(((right, 5), (left, 6), (opposite, 7))):
                copy_to(
                    rbuf.at[0, 1 - yh, x], rbuf.at[0, 1 - yh, x], s_src.at[4 + n], r_rz.at[at], target
                ).start()

        cl = lax.rem(kappa, 2)
        for n in range(2):
            near_n = near(4 * hh + xs, 4 * n + x, 1 - lo)
            role_n = jnp.where(kappa == 2, near_n, kappa // 3)
            skip = jnp.logical_or(
                jnp.logical_and(kappa == 0, near_n == 0), jnp.logical_and(kappa == 4, near_n == 1)
            )

            @pl.when(jnp.logical_not(skip))
            def _(n=n, role_n=role_n):
                copy_to(
                    piece, xbuf.at[cl, hh, xs, share], s_y.at[n * 32 + lax.rem(t, 32)],
                    r_y.at[cl * 8 + hh * 4 + xs], dev(z, n, x, 1 - lo, role_n),
                ).start()

    def forward_pair(c):
        products = []
        for panel in (c - 1, c):
            cl, hh, xs = forward_place(panel)
            at = cl * 8 + hh * 4 + xs
            wait_bytes(xbuf.at[cl, hh, xs, pl.ds(AR, 4 * RB)], r_y.at[at])
            products.append((at, cl, hh, xs))
        total = acc[...]
        for at, cl, hh, xs in products:
            total = total + jnp.dot(dense[at], xbuf[cl, hh, xs], preferred_element_type=F32)
        acc[...] = total

    def got_z0(o, s, hh):
        piece = zbuf.at[0, hh, halves[s]]
        role_cond = far_role if o == 0 else None
        wait_recv(piece, r_z0[o][s])
        start(piece, xbuf.at[1, hh, x, halves[s]], r_z1[o][s], ahead, role_cond=role_cond)
        comp_direct(o, s, hh, 0, piece, role_cond)

    def got_z1(o, s, hh):
        piece = xbuf.at[1, hh, x, halves[s]]
        wait_recv(piece, r_z1[o][s])
        start(piece, zbuf.at[1, hh, halves[s]], r_z2[o][s], ahead)
        start(piece, piece, r_dir[1][o][s][0], right)
        start(piece, piece, r_dir[1][o][s][1], left)

    def got_z2(o, s, hh):
        piece = zbuf.at[1, hh, halves[s]]
        wait_recv(piece, r_z2[o][s])
        start(piece, zbuf.at[0, hh, halves[s]], r_z0[o][s], mate, role_cond=near_role)
        comp_direct(o, s, hh, 1, piece)
        own = near(4 * hh + x, w)
        xbuf[0, hh, x, halves[s], :] = zbuf[1 - own, hh, halves[s], :]

    def pass_opposite(cl, o, s, hh):
        whole = cl == 0 and o == 0
        cond = inner if whole else None
        for side, (xs, target) in enumerate(((xl, right), (xr, left))):
            piece = xbuf.at[cl, hh, xs, halves[s]]
            wait_recv(piece, r_dir[cl][o][s][side])
            if whole or s == side:
                start(piece, piece, r_opp[cl][o][s], target, cond=cond)

    def wait_opposite(cl, o, s, hh):
        wait_recv(xbuf.at[cl, hh, xo, halves[s]], r_opp[cl][o][s])

    def by_role(near_at, far_at):
        return jnp.where(near_role, near_at, far_at)

    events = [
        (-1, 12, lambda: got_z0(0, 0, order[0])),
        (38, 43, lambda: wait_opposite(0, 1, 1, order[1])),
        (4, 15, lambda: got_z0(1, 0, order[1])),
        (4, 17, lambda: got_z0(1, 1, order[1])),
        (4, 18, lambda: got_z1(0, 0, order[0])),
        (25, 36, lambda: pass_opposite(0, 1, 1, order[1])),
        (7, 23, lambda: got_z1(1, 0, order[1])),
        (14, 27, lambda: got_z2(1, 0, order[1])),
        (11, 24, lambda: got_z2(0, 0, order[0])),
        (11, 24, lambda: got_z2(0, 1, order[0])),
        (9, 23, lambda: got_z1(1, 1, order[1])),
        (16, 30, lambda: got_z2(1, 1, order[1])),
        (12, 28, lambda: pass_opposite(1, 0, 0, order[0])),
        (13, 30, lambda: pass_opposite(1, 0, 1, order[0])),
        (4, 21, lambda: got_z1(0, 1, order[0])),
        (17, 32, lambda: pass_opposite(1, 1, 1, order[1])),
        (29, 37, lambda: wait_opposite(1, 1, 0, order[1])),
        (16, 30, lambda: pass_opposite(1, 1, 0, order[1])),
        (24, 39, lambda: pass_opposite(0, 1, 0, order[1])),
        (19, 35, lambda: pass_opposite(0, 0, 1, order[0])),
        (23, 36, lambda: wait_opposite(1, 0, 1, order[0])),
        (24, 35, lambda: wait_opposite(1, 0, 0, order[0])),
        (28, 33, lambda: pass_opposite(0, 0, 0, order[0])),
        (26, 37, lambda: wait_opposite(1, 1, 1, order[1])),
        (35, 39, lambda: wait_opposite(0, 0, 0, order[0])),
        (-1, 14, lambda: got_z0(0, 1, order[0])),
        (32, 45, lambda: wait_opposite(0, 1, 0, order[1])),
        (30, 40, lambda: wait_opposite(0, 0, 1, order[0])),
    ]
    compute_from = by_role(24, 31)

    def forward_step(t, carry):
        for near_at, far_at, what in events:
            pl.when(t == by_role(near_at, far_at))(what)

        @pl.when(t < 40)
        def _():
            relay_forward(t)

        @pl.when(t == BUILD_FROM)
        def _():
            load_w.wait()

        @pl.when(jnp.logical_and(t >= BUILD_FROM, t < BUILD_FROM + 16))
        def _():
            build(t - BUILD_FROM)

        c = t - compute_from

        @pl.when(jnp.logical_and(jnp.logical_and(c >= 0, c < 16), lax.rem(c, 2) == 1))
        def _():
            forward_pair(c)

        return carry

    lax.fori_loop(0, FWD_STEPS, forward_step, 0)

    mid_src[...] = acc[...].astype(BF16)
    r_mid, r_sc = recv_slot(3), recv_slot(3)
    core_mate, chip_mate = (i, 2 * lo + 1 - core), (i, 2 * (1 - lo) + core)

    def quarter_rows(lo_, core_):
        return pl.ds(pl.multiple_of((2 * lo_ + core_) * QR, QR), QR)

    for lo_ in (1 - lo, lo):
        start(mid_src.at[quarter_rows(lo_, 1 - core)], mid_in.at[lo_], r_mid + lo_, core_mate)
    wait_recv(mid_in.at[1 - lo], r_mid + 1 - lo)
    mid_out[...] = (
        acc[quarter_rows(1 - lo, core), :] + mid_in[1 - lo].astype(F32)
    ).astype(BF16)
    start(mid_out, mid_in.at[2], r_mid + 2, chip_mate)
    own_rows = pl.ds(pl.multiple_of(r * QR, QR), QR)
    load_self.wait()
    load_neigh.wait()
    total = acc[own_rows, :]
    f_own = feat[own_rows, :]
    divisor = jnp.concatenate([dcol[own_rows, :], dcol[own_rows, :]], axis=1)
    preact = jnp.dot(f_own, wself[...], preferred_element_type=F32) + bias[...].astype(F32)[None, :]
    load_cot.wait()
    wait_recv(mid_in.at[lo], r_mid + lo)
    total = total + mid_in[lo].astype(F32)
    wait_recv(mid_in.at[2], r_mid + 2)
    total = total + mid_in[2].astype(F32)
    neighbours = (total / divisor).astype(BF16)
    preact = preact + jnp.dot(neighbours, wneigh[...], preferred_element_type=F32)
    sig = jax.nn.sigmoid(preact)
    slope = sig * (1.0 + preact * (1.0 - sig))
    pre_grad = (cot[...].astype(F32) * slope).astype(BF16)
    contract = (((1,), (1,)), ((), ()))
    scaled = lax.dot_general(pre_grad, wneigh[...], contract, preferred_element_type=F32)
    sbuf[own_rows, :] = (scaled / divisor).astype(BF16)
    start(sbuf.at[own_rows], sbuf.at[own_rows], r_sc, chip_mate)
    start(sbuf.at[own_rows], sbuf.at[own_rows], r_sc + 1, core_mate)
    both[:, 0:HID] = (preact * sig).astype(BF16)
    base[...] = lax.dot_general(pre_grad, wself[...], contract, preferred_element_type=F32)
    passed_on = sbuf.at[quarter_rows(1 - lo, core)]
    wait_recv(passed_on, r_sc)
    start(passed_on, passed_on, r_sc + 2, core_mate)
    wait_recv(sbuf.at[quarter_rows(lo, 1 - core)], r_sc + 1)
    wait_recv(sbuf.at[quarter_rows(1 - lo, 1 - core)], r_sc + 2)
    sflip[...] = sbuf[...].T

    b_opp = [[recv_slot(2) for o in range(2)] for cl in range(2)]
    b_dir = [[[recv_slot() for _ in range(2)] for _ in order] for _ in range(2)]
    b_chain = slots_for(3, 2, 2)
    r_fa = recv_slot(4)
    mine = 2 * lo + yh
    far_opp_side = jnp.where(x <= 1, 0, 1)
    far_opp_to = dev(z, yh, jnp.where(x <= 1, xr, xl), lo, role)

    def backward_panel(c):
        cl = jnp.where(c < 8, 0, 1)
        m = lax.rem(c, 8)
        hh, n = lax.rem(m, 2), m // 2
        xs = lax.rem(x + jnp.where(n == 0, 2, jnp.where(n == 1, 3, jnp.where(n == 2, 1, 0))), 4)
        at = cl * 8 + hh * 4 + xs
        flipped = jnp.dot(sflip[...], dense[at], preferred_element_type=F32)
        pbuf[cl, hh, xs] = flipped.astype(BF16).T
        for q in range(4):
            copy_to(
                pbuf.at[cl, hh, xs, pl.ds(AR + RB * q, RB)], rin.at[yh, role, cl, hh, xs],
                s_p.at[at * 4 + q], r_p.at[(yh * 2 + role) * 16 + at],
                dev(z, q // 2, x, 1 - lo, q % 2),
            ).start()

    def relay_backward(u):
        kappa, idx = 4 - u // 8, lax.rem(u, 8)
        hh, n = lax.rem(idx, 2), idx // 2
        xs = lax.rem(x + jnp.where(n == 0, 2, jnp.where(n == 1, 3, jnp.where(n == 2, 1, 0))), 4)
        cl = lax.rem(kappa, 2)
        tacc[...] = jnp.zeros_like(tacc)
        for n in range(2):
            near_n = near(4 * hh + xs, 4 * n + x, 1 - lo)
            role_n = jnp.where(kappa == 2, near_n, kappa // 3)
            skip = jnp.logical_or(
                jnp.logical_and(kappa == 0, near_n == 0), jnp.logical_and(kappa == 4, near_n == 1)
            )

            @pl.when(jnp.logical_not(skip))
            def _(n=n, role_n=role_n):
                wait_bytes(
                    rin.at[n, role_n, cl, hh, xs], r_p.at[(n * 2 + role_n) * 16 + cl * 8 + hh * 4 + xs]
                )
                tacc[...] += rin[n, role_n, cl, hh, xs].astype(F32)

        @pl.when(u >= 8)
        def _():
            wait_bytes(tin.at[kappa, hh, xs], r_t.at[u - 8])
            tacc[...] += tin[kappa, hh, xs].astype(F32)

        tout[kappa, hh, xs] = tacc[...].astype(BF16)

        @pl.when(u < 32)
        def _():
            copy_to(tout.at[kappa, hh, xs], tin.at[kappa - 1, hh, xs], s_t.at[u], r_t.at[u], ahead).start()

        @pl.when(u >= 32)
        def _():
            final_relay(idx, hh, xs, True)

    def final_relay(idx, hh, xs, begin):
        source = lo * 4 + x
        for q in range(4):
            for part, (a, rows, quarter, at) in enumerate(B_PARTS[q]):
                here = jnp.logical_and(
                    jnp.logical_and(hh == yh, xs == x), jnp.logical_and(r == quarter, relay == q)
                )
                gone = jnp.logical_and(relay == q, jnp.logical_not(here))
                src, dst = tout.at[0, hh, xs, pl.ds(a, rows)], fin_b.at[source, pl.ds(at, rows)]
                send_sem = s_fb.at[idx * 2 + part]
                if begin:
                    @pl.when(gone)
                    def _(src=src, dst=dst, send_sem=send_sem, quarter=quarter):
                        copy_to(
                            src, dst, send_sem, r_fb.at[source], (z * 8 + hh * 4 + xs, quarter)
                        ).start()

                    @pl.when(here)
                    def _(src=src, dst=dst):
                        pltpu.make_async_copy(src, dst, r_fb.at[source]).start()
                else:
                    @pl.when(gone)
                    def _(src=src, send_sem=send_sem):
                        wait_bytes(src, send_sem)

    def send_opposite(cl):
        for o, hh in enumerate(order):
            if cl == 0 and o == 0:
                start(
                    pbuf.at[cl, hh, xo, arows], opp_in.at[cl, o, far_opp_side],
                    b_opp[cl][o] + far_opp_side, far_opp_to,
                )
            else:
                start(pbuf.at[cl, hh, xo, low], opp_in.at[cl, o, 1, low], b_opp[cl][o] + 1, left)
                start(pbuf.at[cl, hh, xo, high], opp_in.at[cl, o, 0, high], b_opp[cl][o], right)

    def send_direct(cl, o, hh):
        def merge(side, xs, part):
            wait_recv(opp_in.at[cl, o, side, part], b_opp[cl][o] + side)
            pbuf[cl, hh, xs, part, :] = (
                pbuf[cl, hh, xs, part, :].astype(F32) + opp_in[cl, o, side, part, :].astype(F32)
            ).astype(BF16)

        if cl == 0 and o == 0:
            @pl.when(inner)
            def _():
                merge(0, xr, arows)
                merge(1, xl, arows)
        else:
            merge(0, xr, high)
            merge(1, xl, low)
        start(pbuf.at[cl, hh, xl, arows], dir_in.at[cl, o, 1], b_dir[cl][o][1], left)
        start(pbuf.at[cl, hh, xr, arows], dir_in.at[cl, o, 0], b_dir[cl][o][0], right)

    def sum_composite(o, hh):
        wait_recv(dir_in.at[0, o, 0], b_dir[0][o][0])
        wait_recv(dir_in.at[0, o, 1], b_dir[0][o][1])
        wp = 4 * hh + x
        n_own = near(wp, w).astype(F32)
        n_left = near(wp, 4 * yh + xl).astype(F32)
        n_right = near(wp, 4 * yh + xr).astype(F32)
        v_own = pbuf[0, hh, x, arows, :].astype(F32)
        v_left = dir_in[0, o, 0].astype(F32)
        v_right = dir_in[0, o, 1].astype(F32)
        znear[o] = n_own * v_own + n_left * v_left + n_right * v_right
        zfar[o] = (1.0 - n_own) * v_own + (1.0 - n_left) * v_left + (1.0 - n_right) * v_right

    def chain_two(o, s):
        half = halves[s]

        @pl.when(far_role)
        def _():
            chain_out[2, o, half, :] = zfar[o, half, :].astype(BF16)

        @pl.when(near_role)
        def _():
            wait_recv(chain_in.at[2, o, half], b_chain[2][o][s])
            chain_out[2, o, half, :] = (
                zfar[o, half, :] + chain_in[2, o, half, :].astype(F32)
            ).astype(BF16)

        start(chain_out.at[2, o, half], chain_in.at[1, o, half], b_chain[1][o][s], behind)

    def sum_whole(o, hh):
        wait_recv(dir_in.at[1, o, 0], b_dir[1][o][0])
        wait_recv(dir_in.at[1, o, 1], b_dir[1][o][1])
        zone[o] = (
            pbuf[1, hh, x, arows, :].astype(F32) + dir_in[1, o, 0].astype(F32) + dir_in[1, o, 1].astype(F32)
        )

    def chain_one(o, s):
        half = halves[s]
        wait_recv(chain_in.at[1, o, half], b_chain[1][o][s])
        chain_out[1, o, half, :] = (
            zone[o, half, :] + chain_in[1, o, half, :].astype(F32)
        ).astype(BF16)
        start(chain_out.at[1, o, half], chain_in.at[0, o, half], b_chain[0][o][s], behind)

    def chain_zero(o, s, hh):
        half = halves[s]
        wait_recv(chain_in.at[0, o, half], b_chain[0][o][s])
        chain_out[0, o, half, :] = (
            znear[o, half, :] + chain_in[0, o, half, :].astype(F32)
        ).astype(BF16)
        start(
            chain_out.at[0, o, half], chain_in.at[2, o, half], b_chain[2][o][s], mate, role_cond=far_role
        )
        for a, rows, quarter, at in A_PARTS[s]:
            src = chain_out.at[0, o, pl.ds(s * HA + a, rows)]
            dst = fin_a.at[mine, pl.ds(at, rows)]
            cond = None
            if o == 0:
                cond = not_quarter[quarter]

                @pl.when(jnp.logical_and(near_role, r == quarter))
                def _(src=src, dst=dst):
                    pltpu.make_async_copy(src, dst, recv_sems.at[r_fa + mine]).start()
            start(
                src, dst, r_fa + mine, (z * 8 + hh * 4 + x, quarter), cond=cond, role_cond=near_role
            )

    late = by_role(5, 0)
    relay_from = by_role(2, 6)
    back_events = [
        (10, 2, lambda: send_opposite(0)),
        (30, 17, lambda: sum_whole(0, yh)),
        (38, 26, lambda: chain_zero(0, 1, yh)),
        (16, 10, lambda: send_opposite(1)),
        (28, 14, lambda: sum_composite(1, 1 - yh)),
        (37, 24, lambda: chain_zero(0, 0, yh)),
        (17, 7, lambda: send_direct(0, 0, yh)),
        (23, 11, lambda: sum_composite(0, yh)),
        (38, 28, lambda: chain_zero(1, 0, 1 - yh)),
        (38, 29, lambda: chain_zero(1, 1, 1 - yh)),
        (28, 16, lambda: chain_two(1, 0)),
        (28, 15, lambda: chain_two(1, 1)),
        (35, 23, lambda: chain_one(1, 0)),
        (35, 24, lambda: chain_one(1, 1)),
        (19, 8, lambda: send_direct(0, 1, 1 - yh)),
        (23, 14, lambda: chain_two(0, 0)),
        (26, 11, lambda: chain_two(0, 1)),
        (25, 15, lambda: send_direct(1, 1, 1 - yh)),
        (20, 14, lambda: send_direct(1, 0, yh)),
        (33, 18, lambda: chain_one(0, 1)),
        (30, 17, lambda: chain_one(0, 0)),
        (34, 22, lambda: sum_whole(1, 1 - yh)),
    ]

    def backward_step(t, carry):
        for near_at, far_at, what in back_events:
            pl.when(t == by_role(near_at, far_at))(what)

        c = t - late

        @pl.when(jnp.logical_and(c >= 0, c < 16))
        def _():
            backward_panel(c)

        u = t - relay_from

        @pl.when(jnp.logical_and(u >= 0, u < 40))
        def _():
            relay_backward(u)

        return carry

    lax.fori_loop(0, BWD_STEPS, backward_step, 0)

    for quarter in range(4):
        a_rows = sum(p[1] for parts in A_PARTS for p in parts if p[2] == quarter)

        @pl.when(r == quarter)
        def _(a_rows=a_rows):
            if a_rows:
                part = pl.ds(0, a_rows)
                for source in range(4):
                    wait_recv(fin_a.at[source, part], r_fa + source)
                result = base[part, :]
                for source in range(4):
                    result = result + fin_a[source, part, :].astype(F32)
                both[part, HID:] = result.astype(BF16)
            if a_rows < QR:
                part = pl.ds(a_rows, QR - a_rows)
                for source in range(8):
                    wait_bytes(fin_b.at[source, part], r_fb.at[source])
                result = base[part, :]
                for source in range(8):
                    result = result + fin_b[source, part, :].astype(F32)
                both[part, HID:] = result.astype(BF16)

    drain()
    drain_many(s_rz, 32, RB)
    drain_many(s_src, 7, RB)
    drain_many(s_y, 64, RB)
    drain_many(s_p, 64, RB)
    drain_many(s_t, 32, RB)

    def drain_final(idx, carry):
        hh, n = lax.rem(idx, 2), idx // 2
        xs = lax.rem(x + jnp.where(n == 0, 2, jnp.where(n == 1, 3, jnp.where(n == 2, 1, 0))), 4)
        final_relay(idx, hh, xs, False)
        return carry

    lax.fori_loop(0, 8, drain_final, 0)


def on_device(
    features, degrees, cotangent, self_weight, neigh_weight, bias_vector,
    block_values, block_rows, block_cols, block_count,
):
    vmem = pl.BlockSpec(memory_space=pltpu.VMEM)
    smem = pl.BlockSpec(memory_space=pltpu.SMEM)
    anyspace = pl.BlockSpec(memory_space=pl.ANY)
    panel = (PR, HID)
    apanel = (AR, HID)
    piece = (RB, HID)
    dma = pltpu.SemaphoreType.DMA
    both = pl.pallas_call(
        kernel,
        out_shape=jax.ShapeDtypeStruct((QR, 2 * HID), BF16),
        in_specs=[smem, smem, smem, anyspace, vmem, anyspace, anyspace, anyspace, vmem, anyspace],
        out_specs=vmem,
        scratch_shapes=[
            pltpu.VMEM(panel, BF16),
            pltpu.VMEM((HID, HID), BF16),
            pltpu.VMEM((HID, HID), BF16),
            pltpu.VMEM((16, SLOTS, BLK, BLK), BF16),
            pltpu.VMEM((16, PR, PR), BF16),
            pltpu.VMEM((SLOTS + 1, BLK, BLK), BF16),
            pltpu.VMEM((2, 2, 4) + panel, BF16),
            pltpu.VMEM((2, 2) + apanel, BF16),
            pltpu.VMEM(panel, F32),
            pltpu.VMEM((QR, HID), BF16),
            pltpu.VMEM((PR, BLK), F32),
            pltpu.VMEM(panel, BF16),
            pltpu.VMEM((3, QR, HID), BF16),
            pltpu.VMEM((QR, HID), BF16),
            pltpu.VMEM(panel, BF16),
            pltpu.VMEM((HID, PR), BF16),
            pltpu.VMEM((QR, HID), F32),
            pltpu.VMEM((5, 2, 4) + piece, BF16),
            pltpu.VMEM((2, 2, 4) + panel, BF16),
            pltpu.VMEM((2, 2, 2) + apanel, BF16),
            pltpu.VMEM((2, 2, 2) + apanel, BF16),
            pltpu.VMEM((2,) + apanel, F32),
            pltpu.VMEM((2,) + apanel, F32),
            pltpu.VMEM((2,) + apanel, F32),
            pltpu.VMEM((3, 2) + apanel, BF16),
            pltpu.VMEM((3, 2) + apanel, BF16),
            pltpu.VMEM((4, QR, HID), BF16),
            pltpu.VMEM((2, 2, 2, 2, 4) + piece, BF16),
            pltpu.VMEM((4, 2, 4) + piece, BF16),
            pltpu.VMEM((5, 2, 4) + piece, BF16),
            pltpu.VMEM(piece, F32),
            pltpu.VMEM((8, QR, HID), BF16),
            dma((128,)),
            dma((128,)),
            dma((5,)),
            pltpu.SemaphoreType.REGULAR,
            dma((32,)),
            dma((40,)),
            dma((7,)),
            dma((64,)),
            dma((16,)),
            dma((64,)),
            dma((64,)),
            dma((32,)),
            dma((32,)),
            dma((16,)),
            dma((8,)),
        ],
        compiler_params=pltpu.CompilerParams(
            collective_id=0, has_side_effects=True, vmem_limit_bytes=62 * 1024 * 1024
        ),
        name="sage_layer",
    )(
        jnp.transpose(block_rows, (2, 0, 1)), jnp.transpose(block_cols, (2, 0, 1)), block_count,
        features, degrees.reshape(NB, BLK), cotangent,
        self_weight, neigh_weight, bias_vector, block_values,
    )
    return both[:, 0:HID], both[:, HID:]


def solution(mesh):
    return jax.shard_map(
        on_device,
        mesh=mesh,
        in_specs=(
            P("rows", None),
            P("rows"),
            P("rows", None),
            P(),
            P(),
            P(),
            P("rows", "rep", None, None, None),
            P("rows", "rep", None),
            P("rows", "rep", None),
            P("rows", "rep"),
        ),
        out_specs=(P(("rows", "rep"), None), P(("rows", "rep"), None)),
        check_vma=False,
    )
```
